512 devices in a mesh: gx: 16 (over x_lo, y), gy: 4 (over x_hi, core), sa: 8 (over z).
Axes of the slice: x: 4 (x_hi: 2, x_lo: 2; x = x_hi * 2 + x_lo), y: 8, z: 8, core: 2. Of those that a mesh axis runs over, the one named last changes fastest.
Arguments:
- trajectory: float32 [2, 32, 36, 256, 512], P(None, 'sa', None, 'gx', 'gy'), may hold values from 0.2 to 2
- adjoint_seed: float32 [32, 36, 256, 512], P('sa', None, 'gx', 'gy'), may hold values from -6 to 6
- wind: float32 [256, 512], P('gx', 'gy'), may hold values from 0.05 to 1
- growth_shape: float32 [32, 36], P('sa'), may hold values from -1 to 1
- group_speeds: float32 [2, 32, 36], P(None, 'sa'), may hold values from 0.05 to 0.45
- upwind_codes: int32 [32, 36], P('sa'), may hold values from 0 to 3
- sea_mask: int32 [256, 512], P('gx', 'gy'), may hold values 0 or 1
- boundary_flags: int32 [256, 512], P('gx', 'gy'), may hold values from 0 to 1, as said below
Outputs:
- state_gradient: float32 [32, 36, 256, 512], P('sa', None, 'gx', 'gy')
- wind_gradient: float32 [256, 512], P('gx', 'gy')
The draws below stay inside these ranges and needn't reach their ends.
Inputs may be any that keep to these rules, and one draw needn't show every extreme that they name: `upwind_codes`: code % 2 == 1: the upwind neighbour along the first grid dimension is the next cell, else the previous; code // 2 likewise along the second. `sea_mask`: 1 for sea, 0 for land. `boundary_flags`: 1 only on cells of the grid's outermost rows and columns.
All inputs are finite; a program needn't handle non-finite values. No bound on the sum of `sea_mask` on one device may be relied on, other than what follows from the above.
Results may differ from the reference program's by a relative error of at most 0.0001.
Values sent between devices are 32-bit elements; how exact they have to be, the bound alone decides.
No kernel may reach another device: no remote copies, remote signals or barrier semaphores. Data moves between devices by JAX's collectives and lax.ppermute only.
A program may use at most 64 MiB of HBM per device.

```python
import math
import jax
import jax.numpy as jnp
from jax import lax

FREQS = 32
DIRS = 36
STEPS = 2
NX = 256
NY = 512


def draw_boundary_flags(key, part):
    key = jax.random.fold_in(key, 7)
    random_bits = jax.random.randint(key, (NX, NY), 0, 2)
    row_index = lax.broadcasted_iota(jnp.int32, (NX, NY), 0)
    col_index = lax.broadcasted_iota(jnp.int32, (NX, NY), 1)
    outer = (row_index == 0) | (row_index == NX - 1) | (col_index == 0) | (col_index == NY - 1)
    return jnp.where(outer, random_bits, 0).astype(jnp.int32)


def with_ends(values, rng, least, high):
    longest = values.shape.index(max(values.shape))
    spots = []
    for shift in (0, 1):
        where = [jax.random.randint(jax.random.fold_in(rng, axis), (), 0, length) for axis, length in enumerate(values.shape)]
        where[longest] = (where[longest] + shift) % values.shape[longest]
        spots.append(tuple(where))
    return values.at[spots[0]].set(least).at[spots[1]].set(high)


def block_levels(rng, shape, pieces, low, largest):
    loudness = 1.0
    for dim, shards_of in pieces:
        draws = jax.random.uniform(jax.random.fold_in(jax.random.fold_in(rng, 6), dim), (shards_of,), jnp.float32, low / len(pieces), largest / len(pieces))
        loudness = loudness * jnp.repeat(jnp.exp(draws), shape[dim] // shards_of).reshape((-1,) + (1,) * (len(shape) - 1 - dim))
    return loudness


def noise(rng, dims, scale, most, shards=(), held_as=jnp.bfloat16):
    loudness = block_levels(rng, dims, shards, -0.22, 0.18) if shards else 1.0
    array = jax.random.normal(rng, dims, jnp.float32) * scale * loudness
    return jnp.minimum(jnp.maximum(array, -most), most).astype(held_as)


def setup_inputs(seed: int = 0) -> dict:
    seeds = jax.random.split(jax.random.key(seed), 9)
    return {
        "trajectory": jnp.clip(jnp.exp(math.log(2.0) - 2.3025851 * jax.random.uniform(seeds[0], (STEPS, FREQS, DIRS, NX, NY), jnp.float32) ** block_levels(seeds[0], (STEPS, FREQS, DIRS, NX, NY), ((1, 8), (3, 16), (4, 4)), -0.2, 0.2)), 0.2, 2.0),
        "adjoint_seed": noise(seeds[1], (FREQS, DIRS, NX, NY), 1.0, 6.0, ((0, 8), (2, 16), (3, 4)), jnp.float32),
        "wind": jnp.clip(jnp.exp(math.log(1.0) - 2.9957323 * jax.random.uniform(seeds[2], (NX, NY), jnp.float32) ** block_levels(seeds[2], (NX, NY), ((0, 16), (1, 4)), -0.2, 0.2)), 0.05, 1.0),
        "growth_shape": jnp.clip(jax.random.uniform(seeds[3], (FREQS, DIRS), jnp.float32, -1.0, 1.0) * block_levels(seeds[3], (FREQS, DIRS), ((0, 8),), -0.4, 0.0), -1.0, 1.0),
        "group_speeds": jnp.clip(0.05 + 0.39999999 * jax.random.uniform(seeds[4], (2, FREQS, DIRS), jnp.float32) ** block_levels(seeds[4], (2, FREQS, DIRS), ((1, 8),), -0.2, 0.2), 0.05, 0.45),
        "upwind_codes": with_ends(jax.random.randint(seeds[5], (FREQS, DIRS), 0, 4), jax.random.fold_in(seeds[5], 1), 0, 3).astype(jnp.int32),
        "sea_mask": with_ends((jax.random.randint(seeds[6], (NX, NY), 0, 8) < 7).astype(jnp.int32), jax.random.fold_in(seeds[6], 1), 0, 1),
        "boundary_flags": draw_boundary_flags(jax.random.fold_in(seeds[8], 71), 0),
    }


steep_scale = 0.05
freq_growth = 1.1

def spectral_tables():
    levels = jnp.arange(FREQS).astype(jnp.float32) - FREQS // 2
    frequency = jnp.power(jnp.float32(freq_growth), levels)
    weights = frequency / jnp.sum(frequency) / DIRS
    return (frequency, weights)

def upwind_tables(codes, speeds):
    bit_x = (codes % 2)[:, :, None, None] == 1
    bit_y = (codes // 2)[:, :, None, None] == 1
    return (bit_x, bit_y, speeds[0][:, :, None, None], speeds[1][:, :, None, None])

def propagate(padded, density, tables, sea, held):
    bit_x, bit_y, speed_x, speed_y = tables
    inflow_x = jnp.where(bit_x, padded[:, :, 2:, 1:-1], padded[:, :, :-2, 1:-1])
    inflow_y = jnp.where(bit_y, padded[:, :, 1:-1, 2:], padded[:, :, 1:-1, :-2])
    moved = density - speed_x * (density - inflow_x) - speed_y * (density - inflow_y)
    return sea * ((1.0 - held) * moved + held * density)

def source(moved, energy, first_moment, wind, growth, frequency):
    mean_freq = first_moment / energy
    steep = steep_scale * energy * mean_freq ** 4
    damping = (steep / (1.0 + steep)) ** 2
    rate = 0.5 * wind * growth[:, :, None, None] - 0.5 * damping * frequency[:, None, None, None] / mean_freq
    return moved * jnp.exp(rate)

def reference(trajectory, adjoint_seed, wind, growth_shape, group_speeds, upwind_codes, sea_mask, boundary_flags):
    frequency, weights = spectral_tables()
    tables = upwind_tables(upwind_codes, group_speeds)
    sea = sea_mask.astype(jnp.float32)
    held = boundary_flags.astype(jnp.float32)

    def advance(density, wind_in):
        padded = jnp.pad(density, ((0, 0), (0, 0), (1, 1), (1, 1)))
        moved = propagate(padded, density, tables, sea, held)
        energy = 1.0 + lax.optimization_barrier(jnp.sum(moved * weights[:, None, None, None], axis=(0, 1)))
        first_moment = 1.0 + lax.optimization_barrier(jnp.sum(moved * (weights * frequency)[:, None, None, None], axis=(0, 1)))
        return source(moved, energy, first_moment, wind_in, growth_shape, frequency)
    cotangent = adjoint_seed
    wind_total = jnp.zeros_like(wind)
    for position in reversed(range(STEPS)):
        _, pullback = jax.vjp(advance, trajectory[position], wind)
        cotangent, wind_part = pullback(cotangent)
        wind_total = wind_total + wind_part
    return (cotangent, wind_total)
```

```python
import functools

import jax
import jax.numpy as jnp
import numpy as np
from jax import lax
from jax.experimental import pallas as pl
from jax.experimental.pallas import tpu as pltpu
from jax.sharding import PartitionSpec as P

FREQS = 32
DIRS = 36
TILE = 8
PACK = 4
F32 = jnp.float32

steep_scale = 0.05
freq_growth = 1.1

frequency_table = np.power(np.float32(freq_growth), np.arange(FREQS, dtype=np.float32) - FREQS // 2)
frequency_table = frequency_table.astype(np.float32)
weight_table = (frequency_table / np.sum(frequency_table) / np.float32(DIRS)).astype(np.float32)

VMEM = pl.BlockSpec(memory_space=pltpu.VMEM)
SMEM = pl.BlockSpec(memory_space=pltpu.SMEM)
HBM = pl.BlockSpec(memory_space=pltpu.HBM)

STAY, FROM_PREV_X, FROM_NEXT_X, FROM_PREV_Y, FROM_NEXT_Y, GROWTH = range(6)


def bin_constants(table, f, local):
    i = lax.axis_index("sa") * local + f
    return table[0, i], table[1, i]


def is_even(axis):
    return lax.rem(lax.axis_index(axis), 2) == 0


def span(t):
    return slice(t * TILE, (t + 1) * TILE)


def lanes_of(shape):
    return lax.broadcasted_iota(jnp.int32, shape, len(shape) - 1)


def tile_frequency(t):
    f = t * TILE // DIRS
    return f, (t * TILE + TILE - 1) // DIRS != f


def low_half():
    return lax.broadcasted_iota(jnp.int32, (TILE, 128), 0) < TILE // 2


def pick(values, t):
    f, mixed = tile_frequency(t)
    return jnp.where(low_half(), values[f], values[f + 1]) if mixed else values[f]


def accumulate(sums, t, value):
    f, mixed = tile_frequency(t)
    if mixed:
        low = low_half()
        sums[f] = sums[f] + jnp.where(low, value, 0.0)
        sums[f + 1] = sums[f + 1] + jnp.where(low, 0.0, value)
    else:
        sums[f] = sums[f] + value


def over_rows(count, body):
    body(0, True, False)

    def inner(r, carry):
        body(r, False, False)
        return carry

    lax.fori_loop(1, count - 1, inner, 0)
    body(count - 1, False, True)


def column_lane(r, t):
    return (t % PACK) * 32 + 2 * r


def pack_columns(packed, value, r, t):
    at = column_lane(r, t)
    lane = lanes_of(value.shape)
    here = (lane == at) | (lane == lax.rem(at + 127, 128))
    g = t // PACK
    packed[g] = jnp.where(here, pltpu.roll(value, at, 1), packed[g])


def join_columns(near, far, out):
    even = is_even("gy")
    for g in range(out.shape[0]):
        before = jnp.where(even, far[g], near[g])
        after = jnp.where(even, near[g], far[g])
        lane = lanes_of(before.shape)
        out[g] = jnp.where(lane % 2 == 0, pltpu.roll(before, 1, 1), pltpu.roll(after, 127, 1))


def along_lanes(value, columns, r, t):
    lane = lanes_of(value.shape)
    at = column_lane(r, t)
    edge = pltpu.roll(columns[t // PACK], lax.rem(128 - at, 128), 1)
    before = jnp.where(lane == 0, edge, pltpu.roll(value, 1, 1))
    after = jnp.where(lane == 127, edge, pltpu.roll(value, 127, 1))
    return before, after


def put_rows(near_rows, far_rows, t, value, first, last):
    even = is_even("gx")
    if first:
        far_rows[span(t), :] = jnp.where(even, value, far_rows[span(t), :])
        near_rows[span(t), :] = value
    if last:
        near_rows[span(t), :] = jnp.where(even, value, near_rows[span(t), :])
        far_rows[span(t), :] = jnp.where(even, far_rows[span(t), :], value)


def row_halo(near_rows, far_rows, t, upper):
    even = is_even("gx")
    near, far = near_rows[span(t), :], far_rows[span(t), :]
    return jnp.where(even, far, near) if upper else jnp.where(even, near, far)


def set_masks(sea, held, masks):
    sea, held = sea[...].astype(F32), held[...].astype(F32)
    masks[0] = sea * (1.0 - held)
    masks[1] = sea * held


def row_of(ref, r):
    return ref[pl.ds(r, 1), :]


def gathered(sums, q):
    rows = sums.shape[1] // TILE
    total = sums[q, pl.ds(0, rows, TILE), :]
    for k in range(1, TILE):
        total = total + sums[q, pl.ds(k, rows, TILE), :]
    return total


def edges_kernel(state, laid, near_rows, far_rows, cols, arrived):
    steps, rows, bins, lanes = laid.shape
    copies = [
        [pltpu.make_async_copy(state.at[s, :, r, :], laid.at[s, r], arrived.at[s, r]) for r in range(rows)]
        for s in range(steps)
    ]
    for r in range(rows):
        for s in range(steps):
            copies[s][r].start()
    packed = [[jnp.zeros((TILE, lanes), F32)] * cols.shape[1] for _ in range(steps)]
    for r in range(rows):
        for s in range(steps):
            copies[s][r].wait()
            for t in range(bins // TILE):
                value = laid[s, r, span(t), :]
                pack_columns(packed[s], value, r, t)
                put_rows(near_rows.at[s], far_rows.at[s], t, value, r == 0, r == rows - 1)
    for s in range(steps):
        for g in range(cols.shape[1]):
            cols[s, g] = packed[s][g]


def seed_kernel(seed, coef, wind, grown, laid, arrived):
    rows, bins, _ = grown.shape
    copies = [pltpu.make_async_copy(seed.at[:, r, :], laid.at[r], arrived.at[r]) for r in range(rows)]
    for copy in copies:
        copy.start()
    for r in range(rows):
        copies[r].wait()
        half_wind = 0.5 * row_of(wind, r)
        for t in range(bins // TILE):
            grown[r, span(t), :] = laid[r, span(t), :] * jnp.exp(half_wind * coef[GROWTH, span(t), :])


def moved_of(laid, near_rows, far_rows, columns, coef, s1, s2, r, t, first, last):
    value = laid[r, span(t), :]
    prev_x = row_halo(near_rows, far_rows, t, True) if first else laid[r - 1, span(t), :]
    next_x = row_halo(near_rows, far_rows, t, False) if last else laid[r + 1, span(t), :]
    prev_y, next_y = along_lanes(value, columns, r, t)
    flow = (
        coef[STAY, span(t), :] * value
        + coef[FROM_PREV_X, span(t), :] * prev_x
        + coef[FROM_NEXT_X, span(t), :] * next_x
        + coef[FROM_PREV_Y, span(t), :] * prev_y
        + coef[FROM_NEXT_Y, span(t), :] * next_y
    )
    return s1 * flow + s2 * value


def forward_kernel(
    local, table, coef, laid, grown, sea, held, near_rows, far_rows, near_cols, far_cols,
    slots, wind_parts, moved_0, masks, columns, sums,
):
    _, rows, bins, _ = laid.shape
    set_masks(sea, held, masks)
    for s in range(2):
        join_columns(near_cols.at[s], far_cols.at[s], columns.at[s])
    zero = jnp.zeros((TILE, 128), F32)

    def body(r, first, last):
        s1, s2 = row_of(masks.at[0], r), row_of(masks.at[1], r)
        parts = [[zero] * local for _ in range(4)]
        for t in range(bins // TILE):
            early, later = (
                moved_of(laid.at[s], near_rows.at[s], far_rows.at[s], columns.at[s], coef, s1, s2, r, t, first, last)
                for s in range(2)
            )
            moved_0[r, span(t), :] = early
            term = grown[r, span(t), :] * later
            values = later, early, term, coef[GROWTH, span(t), :] * term
            for part, value in zip(parts, values):
                accumulate(part, t, value)
        at = r * TILE if isinstance(r, int) else pl.multiple_of(r * TILE, TILE)
        for i, part in enumerate(parts):
            for f in range(local):
                sums[i * local + f, pl.ds(at, TILE), :] = part[f]

    over_rows(rows, body)
    totals = [jnp.zeros((rows, 128), F32)] * 4
    for f in range(local):
        freq, weight = bin_constants(table, f, local)
        later, early = gathered(sums, f), gathered(sums, local + f)
        terms = weight * later, weight * freq * later, weight * early, weight * freq * early
        totals = [total + term for total, term in zip(totals, terms)]
        wind_parts[f] = gathered(sums, 3 * local + f)
    totals = totals + [gathered(sums, 2 * local + f) for f in range(local)]
    for i, value in enumerate(totals):
        for peer in range(slots.shape[0]):
            slots[peer, i] = value


def rates(energy, first):
    mean_freq = first / energy
    steep = steep_scale * energy * mean_freq**4
    inverse = 1.0 / (1.0 + steep)
    damping = (steep * inverse) ** 2
    q = damping / mean_freq
    return q, q / energy * (1.0 - 6.0 * inverse), q / first * (8.0 * inverse - 1.0)


def set_rates(local, table, q, by_energy, by_first, decays, rests):
    for f in range(local):
        freq, weight = bin_constants(table, f, local)
        decays[f] = jnp.exp((-0.5 * freq) * q)
        rests[f] = weight * by_energy + (weight * freq) * by_first


def lam_rows(local, source, masks, decays, rests, lam, near_rows, far_rows, cols, packed):
    rows, bins, _ = lam.shape
    for g in range(packed.shape[0]):
        packed[g] = jnp.zeros((TILE, 128), F32)

    def body(r, first, last):
        s1 = row_of(masks.at[0], r)
        decay = [row_of(decays.at[f], r) for f in range(local)]
        rest = [row_of(rests.at[f], r) for f in range(local)]
        columns = [packed[g] for g in range(packed.shape[0])]
        for t in range(bins // TILE):
            value = source[r, span(t), :] * pick(decay, t) + pick(rest, t)
            lam[r, span(t), :] = value
            flow = s1 * value
            pack_columns(columns, flow, r, t)
            put_rows(near_rows, far_rows, t, flow, first, last)
        for g in range(packed.shape[0]):
            packed[g] = columns[g]

    over_rows(rows, body)
    for g in range(packed.shape[0]):
        cols[g] = packed[g]


def lam_1_kernel(
    local, table, grown, sea, held, got, wind_parts,
    lam, wind_1, cells, near_rows, far_rows, cols, masks, decays, rests, packed,
):
    peers = got.shape[0]
    set_masks(sea, held, masks)

    def total(i):
        value = got[0, i]
        for peer in range(1, peers):
            value = value + got[peer, i]
        return value

    q, by_energy, by_first = rates(1.0 + total(0), 1.0 + total(1))
    cells[0], cells[1], cells[2] = rates(1.0 + total(2), 1.0 + total(3))
    lam_q = jnp.zeros_like(q)
    for peer in range(peers):
        for f in range(local):
            freq = float(frequency_table[peer * local + f])
            lam_q = lam_q + (-0.5 * freq) * jnp.exp((-0.5 * freq) * q) * got[peer, 4 + f]
    set_rates(local, table, q, lam_q * by_energy, lam_q * by_first, decays, rests)
    wind = jnp.zeros_like(q)
    for f in range(local):
        wind = wind + 0.5 * decays[f] * wind_parts[f]
    wind_1[...] = wind
    lam_rows(local, grown, masks, decays, rests, lam, near_rows, far_rows, cols, packed)


def back_of(lam, near_rows, far_rows, columns, coef, masks, r, t, first, last):
    value = lam[r, span(t), :]
    flow = row_of(masks.at[0], r) * value
    if first:
        prev_x = row_halo(near_rows, far_rows, t, True)
    else:
        prev_x = row_of(masks.at[0], r - 1) * lam[r - 1, span(t), :]
    if last:
        next_x = row_halo(near_rows, far_rows, t, False)
    else:
        next_x = row_of(masks.at[0], r + 1) * lam[r + 1, span(t), :]
    prev_y, next_y = along_lanes(flow, columns, r, t)
    return (
        row_of(masks.at[1], r) * value
        + coef[STAY, span(t), :] * flow
        + coef[FROM_NEXT_X, span(t), :] * prev_x
        + coef[FROM_PREV_X, span(t), :] * next_x
        + coef[FROM_NEXT_Y, span(t), :] * prev_y
        + coef[FROM_PREV_Y, span(t), :] * next_y
    )


def back_1_kernel(
    local, table, coef, lam, moved_0, wind, sea, held, cells, wind_1, near_rows, far_rows, near_cols, far_cols,
    grown, slots, masks, columns, decays, sums,
):
    rows, bins, _ = lam.shape
    set_masks(sea, held, masks)
    join_columns(near_cols, far_cols, columns)
    for f in range(local):
        freq, _ = bin_constants(table, f, local)
        decay = jnp.exp((-0.5 * freq) * cells[0])
        decays[f] = (-0.5 * freq) * decay
        decays[local + f] = 0.5 * decay
    zero = jnp.zeros((TILE, 128), F32)

    def body(r, first, last):
        half_wind = 0.5 * row_of(wind, r)
        for_q = [row_of(decays.at[f], r) for f in range(local)]
        for_wind = [row_of(decays.at[local + f], r) for f in range(local)]
        lam_q, lam_wind = zero, zero
        for t in range(bins // TILE):
            density = back_of(lam, near_rows, far_rows, columns, coef, masks, r, t, first, last)
            g = coef[GROWTH, span(t), :]
            density = density * jnp.exp(half_wind * g)
            grown[r, span(t), :] = density
            term = density * moved_0[r, span(t), :]
            lam_q = lam_q + pick(for_q, t) * term
            lam_wind = lam_wind + pick(for_wind, t) * (g * term)
        at = r * TILE if isinstance(r, int) else pl.multiple_of(r * TILE, TILE)
        sums[0, pl.ds(at, TILE), :] = lam_q
        sums[1, pl.ds(at, TILE), :] = lam_wind

    over_rows(rows, body)
    lam_q, lam_wind = gathered(sums, 0), gathered(sums, 1) + wind_1[...]
    for peer in range(slots.shape[0]):
        slots[peer, 0] = lam_q
        slots[peer, 1] = lam_wind


def lam_0_kernel(
    local, table, grown, sea, held, cells, got,
    lam, wind_total, near_rows, far_rows, cols, masks, decays, rests, packed,
):
    set_masks(sea, held, masks)
    lam_q, lam_wind = got[0, 0], got[0, 1]
    for peer in range(1, got.shape[0]):
        lam_q, lam_wind = lam_q + got[peer, 0], lam_wind + got[peer, 1]
    wind_total[...] = lam_wind
    set_rates(local, table, cells[0], lam_q * cells[1], lam_q * cells[2], decays, rests)
    lam_rows(local, grown, masks, decays, rests, lam, near_rows, far_rows, cols, packed)


def back_0_kernel(
    coef, lam, sea, held, near_rows, far_rows, near_cols, far_cols, out, laid, masks, columns, sent
):
    rows, bins, _ = lam.shape
    set_masks(sea, held, masks)
    join_columns(near_cols, far_cols, columns)
    copies = [pltpu.make_async_copy(laid.at[r], out.at[:, r, :], sent.at[r]) for r in range(rows)]
    for r in range(rows):
        for t in range(bins // TILE):
            laid[r, span(t), :] = back_of(
                lam, near_rows, far_rows, columns, coef, masks, r, t, r == 0, r == rows - 1
            )
        copies[r].start()
    for copy in copies:
        copy.wait()


def swap(near, far, axis):
    count = lax.axis_size(axis)

    def pairs(first):
        return [(i + a, i + 1 - a) for i in range(first, count - 1, 2) for a in (0, 1)]

    return lax.ppermute(near, axis, pairs(0)), lax.ppermute(far, axis, pairs(1))


def exchange(near_rows, far_rows, cols):
    return *swap(near_rows, far_rows, "gx"), *swap(cols, cols, "gy")


def call(body, outs, specs, *args, out_specs=None, scratch=(), us=2, mib=40):
    return pl.pallas_call(
        body,
        out_shape=[jax.ShapeDtypeStruct(shape, F32) for shape in outs],
        in_specs=specs,
        out_specs=out_specs or [VMEM] * len(outs),
        scratch_shapes=list(scratch),
        cost_estimate=pl.CostEstimate(flops=us * 1000000, bytes_accessed=us * 1000000, transcendentals=0),
        compiler_params=pltpu.CompilerParams(vmem_limit_bytes=mib * 1024 * 1024),
    )(*args)


def scratch(*shape):
    return pltpu.VMEM(shape, F32)


def coefficients(growth, speed, code):
    x, y = speed[0], speed[1]
    next_x, next_y = code % 2 == 1, code // 2 == 1
    values = [
        1.0 - x - y,
        jnp.where(next_x, 0.0, x),
        jnp.where(next_x, x, 0.0),
        jnp.where(next_y, 0.0, y),
        jnp.where(next_y, y, 0.0),
        growth,
    ]
    values = jnp.stack(values).reshape(len(values), -1, 1)
    return jnp.broadcast_to(values, values.shape[:2] + (128,))


def shards(trajectory, adjoint_seed, wind, growth, speed, code, sea, held):
    steps, local, dirs, nx, ny = trajectory.shape
    bins = local * dirs
    peers = lax.axis_size("sa")
    groups = -(-bins // (TILE * PACK))
    table = jnp.asarray(np.stack([frequency_table, weight_table]))

    rows, cols, whole, cell = (bins, ny), (groups, TILE, ny), (nx, bins, ny), (nx, ny)
    edges = [rows, rows, cols]
    masks, columns = scratch(2, *cell), scratch(*cols)
    decays, rests, packed = scratch(local, *cell), scratch(local, *cell), scratch(*cols)

    laid, *edge = call(
        edges_kernel,
        [(steps,) + shape for shape in [whole] + edges],
        [HBM],
        trajectory.reshape(steps, bins, nx, ny),
        scratch=[pltpu.SemaphoreType.DMA((steps, nx))],
        mib=40,
    )
    coef = coefficients(growth, speed, code)
    (grown,) = call(
        seed_kernel,
        [whole],
        [HBM, VMEM, VMEM],
        adjoint_seed.reshape(bins, nx, ny), coef, wind,
        scratch=[scratch(*whole), pltpu.SemaphoreType.DMA((nx,))],
    )
    halos = exchange(*edge)
    slots, wind_parts, moved_0 = call(
        functools.partial(forward_kernel, local),
        [(peers, 4 + local) + cell, (local,) + cell, whole],
        [SMEM] + [VMEM] * 9,
        table, coef, laid, grown, sea, held, *halos,
        scratch=[masks, scratch(steps, *cols), scratch(4 * local, nx * TILE, ny)],
    )
    got = lax.all_to_all(slots, "sa", 0, 0)
    lam, wind_1, cells, *edge = call(
        functools.partial(lam_1_kernel, local),
        [whole, cell, (3,) + cell] + edges,
        [SMEM] + [VMEM] * 5,
        table, grown, sea, held, got, wind_parts,
        scratch=[masks, decays, rests, packed],
    )
    halos = exchange(*edge)
    grown, slots = call(
        functools.partial(back_1_kernel, local),
        [whole, (peers, 2) + cell],
        [SMEM] + [VMEM] * 12,
        table, coef, lam, moved_0, wind, sea, held, cells, wind_1, *halos,
        scratch=[masks, columns, scratch(2 * local, *cell), scratch(2, nx * TILE, ny)],
    )
    got = lax.all_to_all(slots, "sa", 0, 0)
    lam, wind_total, *edge = call(
        functools.partial(lam_0_kernel, local),
        [whole, cell] + edges,
        [SMEM] + [VMEM] * 5,
        table, grown, sea, held, cells, got,
        scratch=[masks, decays, rests, packed],
    )
    halos = exchange(*edge)
    (out,) = call(
        back_0_kernel,
        [(bins, nx, ny)],
        [VMEM] * 8,
        coef, lam, sea, held, *halos,
        out_specs=[HBM],
        scratch=[scratch(*whole), masks, columns, pltpu.SemaphoreType.DMA((nx,))],
    )
    return out.reshape(local, dirs, nx, ny), wind_total


def solution(mesh):
    return jax.shard_map(
        shards,
        mesh=mesh,
        in_specs=(
            P(None, "sa", None, "gx", "gy"),
            P("sa", None, "gx", "gy"),
            P("gx", "gy"),
            P("sa", None),
            P(None, "sa", None),
            P("sa", None),
            P("gx", "gy"),
            P("gx", "gy"),
        ),
        out_specs=(P("sa", None, "gx", "gy"), P("gx", "gy")),
        check_vma=False,
    )
```

```python
import functools

import jax
import jax.numpy as jnp
import numpy as np
from jax import lax
from jax.experimental import pallas as pl
from jax.experimental.pallas import tpu as pltpu
from jax.sharding import PartitionSpec as P

FREQS = 32
DIRS = 36
TILE = 8
PACK = 4
WAITS = 4
F32 = jnp.float32

steep_scale = 0.05
freq_growth = 1.1

frequency_table = np.power(np.float32(freq_growth), np.arange(FREQS, dtype=np.float32) - FREQS // 2)
frequency_table = frequency_table.astype(np.float32)
weight_table = (frequency_table / np.sum(frequency_table) / np.float32(DIRS)).astype(np.float32)

VMEM = pl.BlockSpec(memory_space=pltpu.VMEM)
SMEM = pl.BlockSpec(memory_space=pltpu.SMEM)
HBM = pl.BlockSpec(memory_space=pltpu.HBM)

STAY, FROM_PREV_X, FROM_NEXT_X, FROM_PREV_Y, FROM_NEXT_Y, GROWTH = range(6)


def bin_constants(table, f, local):
    i = lax.axis_index("sa") * local + f
    return table[0, i], table[1, i]


def is_even(axis):
    return lax.rem(lax.axis_index(axis), 2) == 0


def span(t):
    return slice(t * TILE, (t + 1) * TILE)


def lanes_of(shape):
    return lax.broadcasted_iota(jnp.int32, shape, len(shape) - 1)


def tile_frequency(t):
    f = t * TILE // DIRS
    return f, (t * TILE + TILE - 1) // DIRS != f


def low_half():
    return lax.broadcasted_iota(jnp.int32, (TILE, 128), 0) < TILE // 2


def pick(values, t):
    f, mixed = tile_frequency(t)
    return jnp.where(low_half(), values[f], values[f + 1]) if mixed else values[f]


def accumulate(sums, t, value):
    f, mixed = tile_frequency(t)
    if mixed:
        low = low_half()
        sums[f] = sums[f] + jnp.where(low, value, 0.0)
        sums[f + 1] = sums[f + 1] + jnp.where(low, 0.0, value)
    else:
        sums[f] = sums[f] + value


def inner_rows(count, body):
    def inner(r, carry):
        body(r, False, False)
        return carry

    lax.fori_loop(1, count - 1, inner, 0)


def outer_rows(count, body):
    body(0, True, False)
    body(count - 1, False, True)


def tile_at(r):
    at = r * TILE if isinstance(r, int) else pl.multiple_of(r * TILE, TILE)
    return pl.ds(at, TILE)


def column_lane(r, t):
    return (t % PACK) * 32 + 2 * r


def pack_columns(packed, value, r, t):
    at = column_lane(r, t)
    lane = lanes_of(value.shape)
    here = (lane == at) | (lane == lax.rem(at + 127, 128))
    g = t // PACK
    packed[g] = jnp.where(here, pltpu.roll(value, at, 1), packed[g])


def join_columns(near, far, out):
    even = is_even("gy")
    for g in range(out.shape[0]):
        before = jnp.where(even, far[g], near[g])
        after = jnp.where(even, near[g], far[g])
        lane = lanes_of(before.shape)
        out[g] = jnp.where(lane % 2 == 0, pltpu.roll(before, 1, 1), pltpu.roll(after, 127, 1))


def along_lanes(value, columns, r, t):
    lane = lanes_of(value.shape)
    at = column_lane(r, t)
    edge = pltpu.roll(columns[t // PACK], lax.rem(128 - at, 128), 1)
    before = jnp.where(lane == 0, edge, pltpu.roll(value, 1, 1))
    after = jnp.where(lane == 127, edge, pltpu.roll(value, 127, 1))
    return before, after


def put_rows(near_rows, far_rows, t, value, first, last):
    even = is_even("gx")
    if first:
        far_rows[span(t), :] = jnp.where(even, value, far_rows[span(t), :])
        near_rows[span(t), :] = value
    if last:
        near_rows[span(t), :] = jnp.where(even, value, near_rows[span(t), :])
        far_rows[span(t), :] = jnp.where(even, far_rows[span(t), :], value)


def row_halo(near_rows, far_rows, t, upper):
    even = is_even("gx")
    near, far = near_rows[span(t), :], far_rows[span(t), :]
    return jnp.where(even, far, near) if upper else jnp.where(even, near, far)


def set_masks(sea, held, masks):
    sea, held = sea[...].astype(F32), held[...].astype(F32)
    masks[0] = sea * (1.0 - held)
    masks[1] = sea * held


def row_of(ref, r):
    return ref[pl.ds(r, 1), :]


def gathered(sums, q):
    rows = sums.shape[1] // TILE
    total = sums[q, pl.ds(0, rows, TILE), :]
    for k in range(1, TILE):
        total = total + sums[q, pl.ds(k, rows, TILE), :]
    return total


def edges_kernel(state, laid, near_rows, far_rows, cols, arrived):
    steps, rows, bins, lanes = laid.shape
    copies = [
        [pltpu.make_async_copy(state.at[s, :, r, :], laid.at[s, r], arrived.at[s, r]) for r in range(rows)]
        for s in range(steps)
    ]
    for r in range(rows):
        for s in range(steps):
            copies[s][r].start()
    packed = [[jnp.zeros((TILE, lanes), F32)] * cols.shape[1] for _ in range(steps)]
    for r in range(rows):
        if r % WAITS == 0:
            for s in range(steps):
                for copy in copies[s][r : r + WAITS]:
                    copy.wait()
        for s in range(steps):
            for t in range(bins // TILE):
                value = laid[s, r, span(t), :]
                pack_columns(packed[s], value, r, t)
                put_rows(near_rows.at[s], far_rows.at[s], t, value, r == 0, r == rows - 1)
    for s in range(steps):
        for g in range(cols.shape[1]):
            cols[s, g] = packed[s][g]


def prepare_kernel(local, growth, speed, code, seed, wind, coef, grown, laid, arrived):
    rows, bins, lanes = grown.shape
    copies = [pltpu.make_async_copy(seed.at[:, r, :], laid.at[r], arrived.at[r]) for r in range(rows)]
    for copy in copies:
        copy.start()

    def fill(d, carry):
        for f in range(local):
            x, y = speed[0, f, d], speed[1, f, d]
            next_x, next_y = lax.rem(code[f, d], 2) == 1, code[f, d] >= 2
            values = [
                1.0 - x - y,
                jnp.where(next_x, 0.0, x),
                jnp.where(next_x, x, 0.0),
                jnp.where(next_y, 0.0, y),
                jnp.where(next_y, y, 0.0),
                growth[f, d],
            ]
            for k, value in enumerate(values):
                coef[k, pl.ds(f * DIRS + d, 1), :] = jnp.full((1, lanes), value, F32)
        return carry

    lax.fori_loop(0, DIRS, fill, 0)
    for r in range(rows):
        if r % WAITS == 0:
            for copy in copies[r : r + WAITS]:
                copy.wait()
        half_wind = 0.5 * row_of(wind, r)
        for t in range(bins // TILE):
            grown[r, span(t), :] = laid[r, span(t), :] * jnp.exp(half_wind * coef[GROWTH, span(t), :])


def moved_of(laid, near_rows, far_rows, columns, coef, s1, s2, r, t, first, last):
    value = laid[r, span(t), :]
    prev_x = row_halo(near_rows, far_rows, t, True) if first else laid[r - 1, span(t), :]
    next_x = row_halo(near_rows, far_rows, t, False) if last else laid[r + 1, span(t), :]
    prev_y, next_y = along_lanes(value, columns, r, t)
    flow = (
        coef[STAY, span(t), :] * value
        + coef[FROM_PREV_X, span(t), :] * prev_x
        + coef[FROM_NEXT_X, span(t), :] * next_x
        + coef[FROM_PREV_Y, span(t), :] * prev_y
        + coef[FROM_NEXT_Y, span(t), :] * next_y
    )
    return s1 * flow + s2 * value


def forward_row(local, coef, laid, grown, masks, halos, columns, sums, moved_0, r, first, last):
    bins = laid.shape[2]
    s1, s2 = row_of(masks.at[0], r), row_of(masks.at[1], r)
    parts = [[jnp.zeros((TILE, 128), F32)] * local for _ in range(4)]
    for t in range(bins // TILE):
        early, later = (
            moved_of(laid.at[s], *(h if h is None else h.at[s] for h in halos), columns.at[s], coef, s1, s2, r, t, first, last)
            for s in range(2)
        )
        moved_0[span(t), :] = early
        term = grown[r, span(t), :] * later
        values = later, early, term, coef[GROWTH, span(t), :] * term
        for part, value in zip(parts, values):
            accumulate(part, t, value)
    for i, part in enumerate(parts):
        for f in range(local):
            sums[i * local + f, tile_at(r), :] = part[f]


def clear_tiles(sums, rows):
    for q in range(sums.shape[0]):
        for r in rows:
            sums[q, tile_at(r), :] = jnp.zeros((TILE, 128), F32)


def inner_forward_kernel(
    local, coef, laid, grown, sea, held, near_cols, far_cols, parts, moved_0, joined, masks, sums
):
    _, rows, _, _ = laid.shape
    set_masks(sea, held, masks)
    for s in range(2):
        join_columns(near_cols.at[s], far_cols.at[s], joined.at[s])
    clear_tiles(sums, (0, rows - 1))

    def body(r, first, last):
        forward_row(local, coef, laid, grown, masks, (None, None), joined, sums, moved_0.at[r], r, first, last)

    inner_rows(rows, body)
    for q in range(parts.shape[0]):
        parts[q] = gathered(sums, q)


def outer_forward_kernel(
    local, table, coef, laid, grown, sea, held, joined, parts, near_rows, far_rows,
    slots, wind_parts, moved_0, masks, sums,
):
    _, rows, _, _ = laid.shape
    set_masks(sea, held, masks)
    clear_tiles(sums, range(1, rows - 1))

    def body(r, first, last):
        halos = near_rows, far_rows
        out = moved_0.at[int(last)]
        forward_row(local, coef, laid, grown, masks, halos, joined, sums, out, r, first, last)

    outer_rows(rows, body)
    totals = [jnp.zeros((rows, 128), F32)] * 4
    for f in range(local):
        freq, weight = bin_constants(table, f, local)
        later, early = (parts[i * local + f] + gathered(sums, i * local + f) for i in range(2))
        terms = weight * later, weight * freq * later, weight * early, weight * freq * early
        totals = [total + term for total, term in zip(totals, terms)]
        wind_parts[f] = parts[3 * local + f] + gathered(sums, 3 * local + f)
    totals = totals + [parts[2 * local + f] + gathered(sums, 2 * local + f) for f in range(local)]
    for i, value in enumerate(totals):
        for peer in range(slots.shape[0]):
            slots[peer, i] = value


def rates(energy, first):
    mean_freq = first / energy
    steep = steep_scale * energy * mean_freq**4
    inverse = 1.0 / (1.0 + steep)
    damping = (steep * inverse) ** 2
    q = damping / mean_freq
    return q, q / energy * (1.0 - 6.0 * inverse), q / first * (8.0 * inverse - 1.0)


def set_rates(local, table, q, by_energy, by_first, decays, rests):
    for f in range(local):
        freq, weight = bin_constants(table, f, local)
        decays[f] = jnp.exp((-0.5 * freq) * q)
        rests[f] = weight * by_energy + (weight * freq) * by_first


def lam_rows(local, source, outer, masks, decays, rests, lam, near_rows, far_rows, cols, packed):
    rows, bins, _ = lam.shape
    for g in range(packed.shape[0]):
        packed[g] = jnp.zeros((TILE, 128), F32)

    def body(r, first, last):
        s1 = row_of(masks.at[0], r)
        decay = [row_of(decays.at[f], r) for f in range(local)]
        rest = [row_of(rests.at[f], r) for f in range(local)]
        columns = [packed[g] for g in range(packed.shape[0])]
        for t in range(bins // TILE):
            known = outer[int(last), span(t), :] if outer is not None and (first or last) else source[r, span(t), :]
            value = known * pick(decay, t) + pick(rest, t)
            lam[r, span(t), :] = value
            flow = s1 * value
            pack_columns(columns, flow, r, t)
            put_rows(near_rows, far_rows, t, flow, first, last)
        for g in range(packed.shape[0]):
            packed[g] = columns[g]

    inner_rows(rows, body)
    outer_rows(rows, body)
    for g in range(packed.shape[0]):
        cols[g] = packed[g]


def lam_1_kernel(
    local, table, grown, sea, held, got, wind_parts,
    lam, wind_1, cells, near_rows, far_rows, cols, masks, decays, rests, packed,
):
    peers = got.shape[0]
    set_masks(sea, held, masks)

    def total(i):
        value = got[0, i]
        for peer in range(1, peers):
            value = value + got[peer, i]
        return value

    q, by_energy, by_first = rates(1.0 + total(0), 1.0 + total(1))
    cells[0], cells[1], cells[2] = rates(1.0 + total(2), 1.0 + total(3))
    lam_q = jnp.zeros_like(q)
    for peer in range(peers):
        for f in range(local):
            freq = float(frequency_table[peer * local + f])
            lam_q = lam_q + (-0.5 * freq) * jnp.exp((-0.5 * freq) * q) * got[peer, 4 + f]
    set_rates(local, table, q, lam_q * by_energy, lam_q * by_first, decays, rests)
    wind = jnp.zeros_like(q)
    for f in range(local):
        wind = wind + 0.5 * decays[f] * wind_parts[f]
    wind_1[...] = wind
    lam_rows(local, grown, None, masks, decays, rests, lam, near_rows, far_rows, cols, packed)


def back_of(lam, near_rows, far_rows, columns, coef, masks, r, t, first, last):
    value = lam[r, span(t), :]
    flow = row_of(masks.at[0], r) * value
    if first:
        prev_x = row_halo(near_rows, far_rows, t, True)
    else:
        prev_x = row_of(masks.at[0], r - 1) * lam[r - 1, span(t), :]
    if last:
        next_x = row_halo(near_rows, far_rows, t, False)
    else:
        next_x = row_of(masks.at[0], r + 1) * lam[r + 1, span(t), :]
    prev_y, next_y = along_lanes(flow, columns, r, t)
    return (
        row_of(masks.at[1], r) * value
        + coef[STAY, span(t), :] * flow
        + coef[FROM_NEXT_X, span(t), :] * prev_x
        + coef[FROM_PREV_X, span(t), :] * next_x
        + coef[FROM_NEXT_Y, span(t), :] * prev_y
        + coef[FROM_PREV_Y, span(t), :] * next_y
    )


def set_decays(local, table, q, decays):
    for f in range(local):
        freq, _ = bin_constants(table, f, local)
        decay = jnp.exp((-0.5 * freq) * q)
        decays[f] = (-0.5 * freq) * decay
        decays[local + f] = 0.5 * decay


def back_row(local, coef, lam, moved_0, wind, masks, halos, columns, decays, sums, grown, r, first, last):
    half_wind = 0.5 * row_of(wind, r)
    for_q = [row_of(decays.at[f], r) for f in range(local)]
    for_wind = [row_of(decays.at[local + f], r) for f in range(local)]
    lam_q = lam_wind = jnp.zeros((TILE, 128), F32)
    for t in range(lam.shape[1] // TILE):
        density = back_of(lam, *halos, columns, coef, masks, r, t, first, last)
        g = coef[GROWTH, span(t), :]
        density = density * jnp.exp(half_wind * g)
        grown[span(t), :] = density
        term = density * moved_0[span(t), :]
        lam_q = lam_q + pick(for_q, t) * term
        lam_wind = lam_wind + pick(for_wind, t) * (g * term)
    sums[0, tile_at(r), :] = lam_q
    sums[1, tile_at(r), :] = lam_wind


def inner_back_1_kernel(
    local, table, coef, lam, moved_0, wind, sea, held, cells, near_cols, far_cols,
    grown, parts, joined, masks, decays, sums,
):
    rows = lam.shape[0]
    set_masks(sea, held, masks)
    join_columns(near_cols, far_cols, joined)
    set_decays(local, table, cells[0], decays)
    clear_tiles(sums, (0, rows - 1))

    def body(r, first, last):
        back_row(
            local, coef, lam, moved_0.at[r], wind, masks, (None, None), joined, decays, sums, grown.at[r], r, first, last
        )

    inner_rows(rows, body)
    for q in range(2):
        parts[q] = gathered(sums, q)


def outer_back_1_kernel(
    local, table, coef, lam, moved_0, wind, sea, held, cells, wind_1, joined, parts, near_rows, far_rows,
    grown, slots, masks, decays, sums,
):
    rows = lam.shape[0]
    set_masks(sea, held, masks)
    set_decays(local, table, cells[0], decays)
    clear_tiles(sums, range(1, rows - 1))

    def body(r, first, last):
        halos = near_rows, far_rows
        i = int(last)
        back_row(
            local, coef, lam, moved_0.at[i], wind, masks, halos, joined, decays, sums, grown.at[i], r, first, last
        )

    outer_rows(rows, body)
    lam_q, lam_wind = parts[0] + gathered(sums, 0), parts[1] + gathered(sums, 1) + wind_1[...]
    for peer in range(slots.shape[0]):
        slots[peer, 0] = lam_q
        slots[peer, 1] = lam_wind


def lam_0_kernel(
    local, table, grown, outer, sea, held, cells, got,
    lam, wind_total, near_rows, far_rows, cols, masks, decays, rests, packed,
):
    set_masks(sea, held, masks)
    lam_q, lam_wind = got[0, 0], got[0, 1]
    for peer in range(1, got.shape[0]):
        lam_q, lam_wind = lam_q + got[peer, 0], lam_wind + got[peer, 1]
    wind_total[...] = lam_wind
    set_rates(local, table, cells[0], lam_q * cells[1], lam_q * cells[2], decays, rests)
    lam_rows(local, grown, outer, masks, decays, rests, lam, near_rows, far_rows, cols, packed)


def send_rows(rows, coef, lam, halos, columns, masks, out, laid, sent):
    count = lam.shape[0]
    copies = []
    for r in rows:
        for t in range(lam.shape[1] // TILE):
            laid[r, span(t), :] = back_of(
                lam, *halos, columns, coef, masks, r, t, r == 0, r == count - 1
            )
        copies.append(pltpu.make_async_copy(laid.at[r], out.at[:, r, :], sent.at[r]))
        copies[-1].start()
    for copy in copies:
        copy.wait()


def inner_back_0_kernel(coef, lam, sea, held, near_cols, far_cols, out, joined, laid, masks, sent):
    set_masks(sea, held, masks)
    join_columns(near_cols, far_cols, joined)
    send_rows(range(1, lam.shape[0] - 1), coef, lam, (None, None), joined, masks, out, laid, sent)


def outer_back_0_kernel(coef, lam, sea, held, joined, near_rows, far_rows, inner, out, laid, masks, sent):
    set_masks(sea, held, masks)
    send_rows((0, lam.shape[0] - 1), coef, lam, (near_rows, far_rows), joined, masks, out, laid, sent)


def swap(near, far, axis):
    count = lax.axis_size(axis)

    def pairs(first):
        return [(i + a, i + 1 - a) for i in range(first, count - 1, 2) for a in (0, 1)]

    return lax.ppermute(near, axis, pairs(0)), lax.ppermute(far, axis, pairs(1))


def exchange(near_rows, far_rows, cols):
    from_columns = swap(cols, cols, "gy")
    return from_columns, swap(near_rows, far_rows, "gx")


def call(body, outs, specs, *args, out_specs=None, scratch=(), us=2, mib=40, aliases=None):
    return pl.pallas_call(
        body,
        out_shape=[jax.ShapeDtypeStruct(shape, F32) for shape in outs],
        in_specs=specs,
        out_specs=out_specs or [VMEM] * len(outs),
        scratch_shapes=list(scratch),
        input_output_aliases=aliases or {},
        cost_estimate=pl.CostEstimate(flops=us * 1000000, bytes_accessed=us * 1000000, transcendentals=0),
        compiler_params=pltpu.CompilerParams(vmem_limit_bytes=mib * 1024 * 1024),
    )(*args)


def scratch(*shape):
    return pltpu.VMEM(shape, F32)


def shards(trajectory, adjoint_seed, wind, growth, speed, code, sea, held):
    steps, local, dirs, nx, ny = trajectory.shape
    bins = local * dirs
    peers = lax.axis_size("sa")
    groups = -(-bins // (TILE * PACK))
    table = jnp.asarray(np.stack([frequency_table, weight_table]))

    rows, cols, whole, cell = (bins, ny), (groups, TILE, ny), (nx, bins, ny), (nx, ny)
    edges = [rows, rows, cols]
    masks = scratch(2, *cell)
    decays, rests, packed = scratch(local, *cell), scratch(local, *cell), scratch(*cols)

    sems, tiles = pltpu.SemaphoreType.DMA((nx,)), nx * TILE

    laid, *edge = call(
        edges_kernel,
        [(steps,) + shape for shape in [whole] + edges],
        [HBM],
        trajectory.reshape(steps, bins, nx, ny),
        scratch=[pltpu.SemaphoreType.DMA((steps, nx))],
    )
    coef, grown = call(
        functools.partial(prepare_kernel, local),
        [(6,) + rows, whole],
        [SMEM] * 3 + [HBM, VMEM],
        growth, speed, code, adjoint_seed.reshape(bins, nx, ny), wind,
        scratch=[scratch(*whole), sems],
    )
    from_columns, from_rows = exchange(*edge)
    parts, moved_0, joined = call(
        functools.partial(inner_forward_kernel, local),
        [(4 * local,) + cell, whole, (steps,) + cols],
        [VMEM] * 7,
        coef, laid, grown, sea, held, *from_columns,
        scratch=[masks, scratch(4 * local, tiles, ny)],
        us=4,
    )
    slots, wind_parts, outer_moved_0 = call(
        functools.partial(outer_forward_kernel, local),
        [(peers, 4 + local) + cell, (local,) + cell, (2,) + rows],
        [SMEM] + [VMEM] * 9,
        table, coef, laid, grown, sea, held, joined, parts, *from_rows,
        scratch=[masks, scratch(4 * local, tiles, ny)],
    )
    got = lax.all_to_all(slots, "sa", 0, 0)
    lam, wind_1, cells, *edge = call(
        functools.partial(lam_1_kernel, local),
        [whole, cell, (3,) + cell] + edges,
        [SMEM] + [VMEM] * 5,
        table, grown, sea, held, got, wind_parts,
        scratch=[masks, decays, rests, packed],
    )
    from_columns, from_rows = exchange(*edge)
    grown, parts, joined = call(
        functools.partial(inner_back_1_kernel, local),
        [whole, (2,) + cell, cols],
        [SMEM] + [VMEM] * 9,
        table, coef, lam, moved_0, wind, sea, held, cells, *from_columns,
        scratch=[masks, scratch(2 * local, *cell), scratch(2, tiles, ny)],
        us=4,
    )
    outer, slots = call(
        functools.partial(outer_back_1_kernel, local),
        [(2,) + rows, (peers, 2) + cell],
        [SMEM] + [VMEM] * 12,
        table, coef, lam, outer_moved_0, wind, sea, held, cells, wind_1, joined, parts, *from_rows,
        scratch=[masks, scratch(2 * local, *cell), scratch(2, tiles, ny)],
    )
    got = lax.all_to_all(slots, "sa", 0, 0)
    lam, wind_total, *edge = call(
        functools.partial(lam_0_kernel, local),
        [whole, cell] + edges,
        [SMEM] + [VMEM] * 6,
        table, grown, outer, sea, held, cells, got,
        scratch=[masks, decays, rests, packed],
    )
    from_columns, from_rows = exchange(*edge)
    inner, joined = call(
        inner_back_0_kernel,
        [(bins, nx, ny), cols],
        [VMEM] * 6,
        coef, lam, sea, held, *from_columns,
        out_specs=[HBM, VMEM],
        scratch=[scratch(*whole), masks, sems],
        us=4,
    )
    (out,) = call(
        outer_back_0_kernel,
        [(bins, nx, ny)],
        [VMEM] * 7 + [HBM],
        coef, lam, sea, held, joined, *from_rows, inner,
        out_specs=[HBM],
        scratch=[scratch(*whole), masks, sems],
        aliases={7: 0},
    )
    return out.reshape(local, dirs, nx, ny), wind_total


def solution(mesh):
    return jax.shard_map(
        shards,
        mesh=mesh,
        in_specs=(
            P(None, "sa", None, "gx", "gy"),
            P("sa", None, "gx", "gy"),
            P("gx", "gy"),
            P("sa", None),
            P(None, "sa", None),
            P("sa", None),
            P("gx", "gy"),
            P("gx", "gy"),
        ),
        out_specs=(P("sa", None, "gx", "gy"), P("gx", "gy")),
        check_vma=False,
    )
```

```python
import functools

import jax
import jax.numpy as jnp
import numpy as np
from jax import lax
from jax.experimental import pallas as pl
from jax.experimental.pallas import tpu as pltpu
from jax.sharding import PartitionSpec as P

FREQS = 32
DIRS = 36
TILE = 8
PACK = 4
WAITS = 4
F32 = jnp.float32

steep_scale = 0.05
freq_growth = 1.1

frequency_table = np.power(np.float32(freq_growth), np.arange(FREQS, dtype=np.float32) - FREQS // 2)
frequency_table = frequency_table.astype(np.float32)
weight_table = (frequency_table / np.sum(frequency_table) / np.float32(DIRS)).astype(np.float32)

VMEM = pl.BlockSpec(memory_space=pltpu.VMEM)
SMEM = pl.BlockSpec(memory_space=pltpu.SMEM)
HBM = pl.BlockSpec(memory_space=pltpu.HBM)

STAY, FROM_PREV_X, FROM_NEXT_X, FROM_PREV_Y, FROM_NEXT_Y, GROWTH = range(6)


def bin_constants(table, f, local):
    i = lax.axis_index("sa") * local + f
    return table[0, i], table[1, i]


def is_even(axis):
    return lax.rem(lax.axis_index(axis), 2) == 0


def span(t):
    return slice(t * TILE, (t + 1) * TILE)


def lanes_of(shape):
    return lax.broadcasted_iota(jnp.int32, shape, len(shape) - 1)


def tile_frequency(t):
    f = t * TILE // DIRS
    return f, (t * TILE + TILE - 1) // DIRS != f


def low_half():
    return lax.broadcasted_iota(jnp.int32, (TILE, 128), 0) < TILE // 2


def pick(values, t):
    f, mixed = tile_frequency(t)
    return jnp.where(low_half(), values[f], values[f + 1]) if mixed else values[f]


def accumulate(sums, t, value):
    f, mixed = tile_frequency(t)
    if mixed:
        low = low_half()
        sums[f] = sums[f] + jnp.where(low, value, 0.0)
        sums[f + 1] = sums[f + 1] + jnp.where(low, 0.0, value)
    else:
        sums[f] = sums[f] + value


def inner_rows(count, body):
    def pair(i, carry):
        body(2 * i + 1, False, False)
        body(2 * i + 2, False, False)
        return carry

    lax.fori_loop(0, (count - 2) // 2, pair, 0)


def outer_rows(count, body):
    body(0, True, False)
    body(count - 1, False, True)


def tile_at(r):
    at = r * TILE if isinstance(r, int) else pl.multiple_of(r * TILE, TILE)
    return pl.ds(at, TILE)


def column_lane(r, t):
    return (t % PACK) * 32 + 2 * r


def pack_columns(packed, value, r, t):
    at = column_lane(r, t)
    lane = lanes_of(value.shape)
    here = (lane == at) | (lane == lax.rem(at + 127, 128))
    g = t // PACK
    packed[g] = jnp.where(here, pltpu.roll(value, at, 1), packed[g])


def join_columns(near, far, out):
    even = is_even("gy")
    for g in range(out.shape[0]):
        before = jnp.where(even, far[g], near[g])
        after = jnp.where(even, near[g], far[g])
        lane = lanes_of(before.shape)
        out[g] = jnp.where(lane % 2 == 0, pltpu.roll(before, 1, 1), pltpu.roll(after, 127, 1))


def along_lanes(value, columns, r, t):
    lane = lanes_of(value.shape)
    at = column_lane(r, t)
    edge = pltpu.roll(columns[t // PACK], lax.rem(128 - at, 128), 1)
    before = jnp.where(lane == 0, edge, pltpu.roll(value, 1, 1))
    after = jnp.where(lane == 127, edge, pltpu.roll(value, 127, 1))
    return before, after


def put_rows(near_rows, far_rows, t, value, first, last):
    even = is_even("gx")
    if first:
        far_rows[span(t), :] = jnp.where(even, value, far_rows[span(t), :])
        near_rows[span(t), :] = value
    if last:
        near_rows[span(t), :] = jnp.where(even, value, near_rows[span(t), :])
        far_rows[span(t), :] = jnp.where(even, far_rows[span(t), :], value)


def row_halo(near_rows, far_rows, t, upper):
    even = is_even("gx")
    near, far = near_rows[span(t), :], far_rows[span(t), :]
    return jnp.where(even, far, near) if upper else jnp.where(even, near, far)


def set_masks(sea, held, masks):
    sea, held = sea[...].astype(F32), held[...].astype(F32)
    masks[0] = sea * (1.0 - held)
    masks[1] = sea * held


def row_of(ref, r):
    return ref[pl.ds(r, 1), :]


def gathered(sums, q):
    rows = sums.shape[1] // TILE
    total = sums[q, pl.ds(0, rows, TILE), :]
    for k in range(1, TILE):
        total = total + sums[q, pl.ds(k, rows, TILE), :]
    return total


def edges_kernel(state, laid, near_rows, far_rows, cols, arrived):
    steps, rows, bins, lanes = laid.shape
    copies = [
        [pltpu.make_async_copy(state.at[s, :, r, :], laid.at[s, r], arrived.at[s, r]) for r in range(rows)]
        for s in range(steps)
    ]
    for r in range(rows):
        for s in range(steps):
            copies[s][r].start()
    packed = [[jnp.zeros((TILE, lanes), F32)] * cols.shape[1] for _ in range(steps)]
    for r in range(rows):
        if r % WAITS == 0:
            for s in range(steps):
                for copy in copies[s][r : r + WAITS]:
                    copy.wait()
        for s in range(steps):
            for t in range(bins // TILE):
                value = laid[s, r, span(t), :]
                pack_columns(packed[s], value, r, t)
                put_rows(near_rows.at[s], far_rows.at[s], t, value, r == 0, r == rows - 1)
    for s in range(steps):
        for g in range(cols.shape[1]):
            cols[s, g] = packed[s][g]


def prepare_kernel(local, growth, speed, code, seed, wind, coef, grown, laid, arrived):
    rows, bins, lanes = grown.shape
    copies = [pltpu.make_async_copy(seed.at[:, r, :], laid.at[r], arrived.at[r]) for r in range(rows)]
    for copy in copies:
        copy.start()

    def fill(d, carry):
        for f in range(local):
            x, y = speed[0, f, d], speed[1, f, d]
            next_x, next_y = lax.rem(code[f, d], 2) == 1, code[f, d] >= 2
            values = [
                1.0 - x - y,
                jnp.where(next_x, 0.0, x),
                jnp.where(next_x, x, 0.0),
                jnp.where(next_y, 0.0, y),
                jnp.where(next_y, y, 0.0),
                growth[f, d],
            ]
            for k, value in enumerate(values):
                coef[k, pl.ds(f * DIRS + d, 1), :] = jnp.full((1, lanes), value, F32)
        return carry

    lax.fori_loop(0, DIRS, fill, 0)
    for r in range(rows):
        if r % WAITS == 0:
            for copy in copies[r : r + WAITS]:
                copy.wait()
        half_wind = 0.5 * row_of(wind, r)
        for t in range(bins // TILE):
            grown[r, span(t), :] = laid[r, span(t), :] * jnp.exp(half_wind * coef[GROWTH, span(t), :])


def moved_of(laid, near_rows, far_rows, columns, coef, s1, s2, r, t, first, last):
    value = laid[r, span(t), :]
    prev_x = row_halo(near_rows, far_rows, t, True) if first else laid[r - 1, span(t), :]
    next_x = row_halo(near_rows, far_rows, t, False) if last else laid[r + 1, span(t), :]
    prev_y, next_y = along_lanes(value, columns, r, t)
    flow = (
        coef[STAY, span(t), :] * value
        + coef[FROM_PREV_X, span(t), :] * prev_x
        + coef[FROM_NEXT_X, span(t), :] * next_x
        + coef[FROM_PREV_Y, span(t), :] * prev_y
        + coef[FROM_NEXT_Y, span(t), :] * next_y
    )
    return s1 * flow + s2 * value


def forward_row(local, coef, laid, grown, masks, halos, columns, sums, moved_0, r, first, last):
    bins = laid.shape[2]
    s1, s2 = row_of(masks.at[0], r), row_of(masks.at[1], r)
    parts = [[jnp.zeros((TILE, 128), F32)] * local for _ in range(4)]
    for t in range(bins // TILE):
        early, later = (
            moved_of(laid.at[s], *(h.at[s] for h in halos), columns.at[s], coef, s1, s2, r, t, first, last)
            for s in range(2)
        )
        moved_0[span(t), :] = early
        term = grown[r, span(t), :] * later
        values = later, early, term, coef[GROWTH, span(t), :] * term
        for part, value in zip(parts, values):
            accumulate(part, t, value)
    for i, part in enumerate(parts):
        for f in range(local):
            sums[i * local + f, tile_at(r), :] = part[f]


def forward_kernel(
    local, table, coef, laid, grown, sea, held, near_cols, far_cols, near_rows, far_rows,
    slots, wind_parts, moved_0, joined, masks, sums,
):
    _, rows, _, _ = laid.shape
    set_masks(sea, held, masks)
    for s in range(2):
        join_columns(near_cols.at[s], far_cols.at[s], joined.at[s])

    def body(r, first, last):
        halos = near_rows, far_rows
        forward_row(local, coef, laid, grown, masks, halos, joined, sums, moved_0.at[r], r, first, last)

    inner_rows(rows, body)
    outer_rows(rows, body)
    totals = [jnp.zeros((rows, 128), F32)] * 4
    for f in range(local):
        freq, weight = bin_constants(table, f, local)
        later, early = gathered(sums, f), gathered(sums, local + f)
        terms = weight * later, weight * freq * later, weight * early, weight * freq * early
        totals = [total + term for total, term in zip(totals, terms)]
        wind_parts[f] = gathered(sums, 3 * local + f)
    totals = totals + [gathered(sums, 2 * local + f) for f in range(local)]
    for i, value in enumerate(totals):
        for peer in range(slots.shape[0]):
            slots[peer, i] = value


def rates(energy, first):
    mean_freq = first / energy
    steep = steep_scale * energy * mean_freq**4
    inverse = 1.0 / (1.0 + steep)
    damping = (steep * inverse) ** 2
    q = damping / mean_freq
    return q, q / energy * (1.0 - 6.0 * inverse), q / first * (8.0 * inverse - 1.0)


def total_of(got, i):
    value = got[0, i]
    for peer in range(1, got.shape[0]):
        value = value + got[peer, i]
    return value


def set_rates(local, table, q, by_energy, by_first, decays, rests):
    for f in range(local):
        freq, weight = bin_constants(table, f, local)
        decays[f] = jnp.exp((-0.5 * freq) * q)
        rests[f] = weight * by_energy + (weight * freq) * by_first


def lam_rows(local, source, masks, decays, rests, lam, near_rows, far_rows, cols, packed):
    rows, bins, _ = lam.shape
    for g in range(packed.shape[0]):
        packed[g] = jnp.zeros((TILE, 128), F32)

    def body(r, first, last):
        s1 = row_of(masks.at[0], r)
        decay = [row_of(decays.at[f], r) for f in range(local)]
        rest = [row_of(rests.at[f], r) for f in range(local)]
        columns = [packed[g] for g in range(packed.shape[0])]
        for t in range(bins // TILE):
            value = source[r, span(t), :] * pick(decay, t) + pick(rest, t)
            lam[r, span(t), :] = value
            flow = s1 * value
            pack_columns(columns, flow, r, t)
            put_rows(near_rows, far_rows, t, flow, first, last)
        for g in range(packed.shape[0]):
            packed[g] = columns[g]

    inner_rows(rows, body)
    outer_rows(rows, body)
    for g in range(packed.shape[0]):
        cols[g] = packed[g]


def lam_1_kernel(
    local, table, grown, sea, held, got, wind_parts,
    lam, wind_1, cells, near_rows, far_rows, cols, masks, decays, rests, packed,
):
    peers = got.shape[0]
    set_masks(sea, held, masks)
    q, by_energy, by_first = rates(1.0 + total_of(got, 0), 1.0 + total_of(got, 1))
    cells[0], cells[1], cells[2] = rates(1.0 + total_of(got, 2), 1.0 + total_of(got, 3))
    lam_q = jnp.zeros_like(q)
    for peer in range(peers):
        for f in range(local):
            freq = float(frequency_table[peer * local + f])
            lam_q = lam_q + (-0.5 * freq) * jnp.exp((-0.5 * freq) * q) * got[peer, 4 + f]
    set_rates(local, table, q, lam_q * by_energy, lam_q * by_first, decays, rests)
    wind = jnp.zeros_like(q)
    for f in range(local):
        wind = wind + 0.5 * decays[f] * wind_parts[f]
    wind_1[...] = wind
    lam_rows(local, grown, masks, decays, rests, lam, near_rows, far_rows, cols, packed)


def back_of(lam, near_rows, far_rows, columns, coef, masks, r, t, first, last):
    value = lam[r, span(t), :]
    flow = row_of(masks.at[0], r) * value
    if first:
        prev_x = row_halo(near_rows, far_rows, t, True)
    else:
        prev_x = row_of(masks.at[0], r - 1) * lam[r - 1, span(t), :]
    if last:
        next_x = row_halo(near_rows, far_rows, t, False)
    else:
        next_x = row_of(masks.at[0], r + 1) * lam[r + 1, span(t), :]
    prev_y, next_y = along_lanes(flow, columns, r, t)
    return (
        row_of(masks.at[1], r) * value
        + coef[STAY, span(t), :] * flow
        + coef[FROM_NEXT_X, span(t), :] * prev_x
        + coef[FROM_PREV_X, span(t), :] * next_x
        + coef[FROM_NEXT_Y, span(t), :] * prev_y
        + coef[FROM_PREV_Y, span(t), :] * next_y
    )


def set_decays(local, table, q, decays):
    for f in range(local):
        freq, _ = bin_constants(table, f, local)
        decay = jnp.exp((-0.5 * freq) * q)
        decays[f] = (-0.5 * freq) * decay
        decays[local + f] = 0.5 * decay


def back_row(local, coef, lam, moved_0, wind, masks, halos, columns, decays, sums, grown, r, first, last):
    half_wind = 0.5 * row_of(wind, r)
    for_q = [row_of(decays.at[f], r) for f in range(local)]
    for_wind = [row_of(decays.at[local + f], r) for f in range(local)]
    lam_q = lam_wind = jnp.zeros((TILE, 128), F32)
    for t in range(lam.shape[1] // TILE):
        density = back_of(lam, *halos, columns, coef, masks, r, t, first, last)
        g = coef[GROWTH, span(t), :]
        density = density * jnp.exp(half_wind * g)
        grown[span(t), :] = density
        term = density * moved_0[span(t), :]
        lam_q = lam_q + pick(for_q, t) * term
        lam_wind = lam_wind + pick(for_wind, t) * (g * term)
    sums[0, tile_at(r), :] = lam_q
    sums[1, tile_at(r), :] = lam_wind


def back_1_kernel(
    local, table, coef, lam, moved_0, wind, sea, held, cells, wind_1,
    near_cols, far_cols, near_rows, far_rows,
    grown, slots, joined, masks, decays, sums,
):
    rows = lam.shape[0]
    set_masks(sea, held, masks)
    join_columns(near_cols, far_cols, joined)
    set_decays(local, table, cells[0], decays)

    def body(r, first, last):
        halos = near_rows, far_rows
        back_row(local, coef, lam, moved_0.at[r], wind, masks, halos, joined, decays, sums, grown.at[r], r, first, last)

    inner_rows(rows, body)
    outer_rows(rows, body)
    lam_q, lam_wind = gathered(sums, 0), gathered(sums, 1) + wind_1[...]
    for peer in range(slots.shape[0]):
        slots[peer, 0] = lam_q
        slots[peer, 1] = lam_wind


def lam_0_kernel(
    local, table, grown, sea, held, cells, got,
    lam, near_rows, far_rows, cols, masks, decays, rests, packed,
):
    set_masks(sea, held, masks)
    lam_q = total_of(got, 0)
    set_rates(local, table, cells[0], lam_q * cells[1], lam_q * cells[2], decays, rests)
    lam_rows(local, grown, masks, decays, rests, lam, near_rows, far_rows, cols, packed)


def back_0_kernel(
    coef, lam, sea, held, got, near_cols, far_cols, near_rows, far_rows, out, wind_total, joined, laid, masks, sent
):
    rows = lam.shape[0]
    set_masks(sea, held, masks)
    join_columns(near_cols, far_cols, joined)
    wind_total[...] = total_of(got, 1)
    copies = [pltpu.make_async_copy(laid.at[r], out.at[:, r, :], sent.at[r]) for r in range(rows)]
    halos = near_rows, far_rows
    for r in range(rows):
        for t in range(lam.shape[1] // TILE):
            laid[r, span(t), :] = back_of(lam, *halos, joined, coef, masks, r, t, r == 0, r == rows - 1)
        copies[r].start()
    for copy in copies:
        copy.wait()


def swap(near, far, axis):
    count = lax.axis_size(axis)

    def pairs(first):
        return [(i + a, i + 1 - a) for i in range(first, count - 1, 2) for a in (0, 1)]

    return lax.ppermute(near, axis, pairs(0)), lax.ppermute(far, axis, pairs(1))


def exchange(near_rows, far_rows, cols):
    from_columns = swap(cols, cols, "gy")
    return from_columns, swap(near_rows, far_rows, "gx")


def call(body, outs, specs, *args, out_specs=None, scratch=(), us=2, mib=40):
    return pl.pallas_call(
        body,
        out_shape=[jax.ShapeDtypeStruct(shape, F32) for shape in outs],
        in_specs=specs,
        out_specs=out_specs or [VMEM] * len(outs),
        scratch_shapes=list(scratch),
        cost_estimate=pl.CostEstimate(flops=us * 1000000, bytes_accessed=us * 1000000, transcendentals=0),
        compiler_params=pltpu.CompilerParams(vmem_limit_bytes=mib * 1024 * 1024),
    )(*args)


def scratch(*shape):
    return pltpu.VMEM(shape, F32)


def shards(trajectory, adjoint_seed, wind, growth, speed, code, sea, held):
    steps, local, dirs, nx, ny = trajectory.shape
    bins = local * dirs
    peers = lax.axis_size("sa")
    groups = -(-bins // (TILE * PACK))
    table = jnp.asarray(np.stack([frequency_table, weight_table]))

    rows, cols, whole, cell = (bins, ny), (groups, TILE, ny), (nx, bins, ny), (nx, ny)
    edges = [rows, rows, cols]
    masks = scratch(2, *cell)
    decays, rests, packed = scratch(local, *cell), scratch(local, *cell), scratch(*cols)

    sems, tiles = pltpu.SemaphoreType.DMA((nx,)), nx * TILE

    laid, *edge = call(
        edges_kernel,
        [(steps,) + shape for shape in [whole] + edges],
        [HBM],
        pltpu.with_memory_space_constraint(trajectory.reshape(steps, bins, nx, ny), pltpu.HBM),
        scratch=[pltpu.SemaphoreType.DMA((steps, nx))],
    )
    coef, grown = call(
        functools.partial(prepare_kernel, local),
        [(6,) + rows, whole],
        [SMEM] * 3 + [HBM, VMEM],
        growth, speed, code, adjoint_seed.reshape(bins, nx, ny), wind,
        scratch=[scratch(*whole), sems],
    )
    from_columns, from_rows = exchange(*edge)
    slots, wind_parts, moved_0 = call(
        functools.partial(forward_kernel, local),
        [(peers, 4 + local) + cell, (local,) + cell, whole],
        [SMEM] + [VMEM] * 9,
        table, coef, laid, grown, sea, held, *from_columns, *from_rows,
        scratch=[scratch(steps, *cols), masks, scratch(4 * local, tiles, ny)],
        us=4,
    )
    got = lax.all_to_all(slots, "sa", 0, 0)
    lam, wind_1, cells, *edge = call(
        functools.partial(lam_1_kernel, local),
        [whole, cell, (3,) + cell] + edges,
        [SMEM] + [VMEM] * 5,
        table, grown, sea, held, got, wind_parts,
        scratch=[masks, decays, rests, packed],
    )
    from_columns, from_rows = exchange(*edge)
    grown, slots = call(
        functools.partial(back_1_kernel, local),
        [whole, (peers, 2) + cell],
        [SMEM] + [VMEM] * 12,
        table, coef, lam, moved_0, wind, sea, held, cells, wind_1, *from_columns, *from_rows,
        scratch=[scratch(*cols), masks, scratch(2 * local, *cell), scratch(2, tiles, ny)],
        us=3,
    )
    got = lax.all_to_all(slots, "sa", 0, 0)
    lam, *edge = call(
        functools.partial(lam_0_kernel, local),
        [whole] + edges,
        [SMEM] + [VMEM] * 5,
        table, grown, sea, held, cells, got,
        scratch=[masks, decays, rests, packed],
    )
    from_columns, from_rows = exchange(*edge)
    out, wind_total = call(
        back_0_kernel,
        [(bins, nx, ny), cell],
        [VMEM] * 9,
        coef, lam, sea, held, got, *from_columns, *from_rows,
        out_specs=[HBM, VMEM],
        scratch=[scratch(*cols), scratch(*whole), masks, sems],
    )
    return out.reshape(local, dirs, nx, ny), wind_total


def solution(mesh):
    return jax.shard_map(
        shards,
        mesh=mesh,
        in_specs=(
            P(None, "sa", None, "gx", "gy"),
            P("sa", None, "gx", "gy"),
            P("gx", "gy"),
            P("sa", None),
            P(None, "sa", None),
            P("sa", None),
            P("gx", "gy"),
            P("gx", "gy"),
        ),
        out_specs=(P("sa", None, "gx", "gy"), P("gx", "gy")),
        check_vma=False,
    )
```

```python
import functools

import jax
import jax.numpy as jnp
import numpy as np
from jax import lax
from jax.experimental import pallas as pl
from jax.experimental.pallas import tpu as pltpu
from jax.sharding import PartitionSpec as P

FREQS = 32
DIRS = 36
TILE = 8
PACK = 4
WAITS = 4
F32 = jnp.float32

steep_scale = 0.05
freq_growth = 1.1

frequency_table = np.power(np.float32(freq_growth), np.arange(FREQS, dtype=np.float32) - FREQS // 2)
frequency_table = frequency_table.astype(np.float32)
weight_table = (frequency_table / np.sum(frequency_table) / np.float32(DIRS)).astype(np.float32)

VMEM = pl.BlockSpec(memory_space=pltpu.VMEM)
SMEM = pl.BlockSpec(memory_space=pltpu.SMEM)
HBM = pl.BlockSpec(memory_space=pltpu.HBM)

STAY, FROM_PREV_X, FROM_NEXT_X, FROM_PREV_Y, FROM_NEXT_Y, GROWTH = range(6)


def bin_constants(table, f, local):
    i = lax.axis_index("sa") * local + f
    return table[0, i], table[1, i]


def is_even(axis):
    return lax.rem(lax.axis_index(axis), 2) == 0


def span(t):
    return slice(t * TILE, (t + 1) * TILE)


def lanes_of(shape):
    return lax.broadcasted_iota(jnp.int32, shape, len(shape) - 1)


def tile_frequency(t):
    f = t * TILE // DIRS
    return f, (t * TILE + TILE - 1) // DIRS != f


def low_half():
    return lax.broadcasted_iota(jnp.int32, (TILE, 128), 0) < TILE // 2


def pick(values, t):
    f, mixed = tile_frequency(t)
    return jnp.where(low_half(), values[f], values[f + 1]) if mixed else values[f]


def accumulate(sums, t, value):
    f, mixed = tile_frequency(t)
    if mixed:
        low = low_half()
        sums[f] = sums[f] + jnp.where(low, value, 0.0)
        sums[f + 1] = sums[f + 1] + jnp.where(low, 0.0, value)
    else:
        sums[f] = sums[f] + value


def inner_rows(count, body):
    def pair(i, carry):
        body(2 * i + 1, False, False)
        body(2 * i + 2, False, False)
        return carry

    lax.fori_loop(0, (count - 2) // 2, pair, 0)


def outer_rows(count, body):
    body(0, True, False)
    body(count - 1, False, True)


def tile_at(r):
    at = r * TILE if isinstance(r, int) else pl.multiple_of(r * TILE, TILE)
    return pl.ds(at, TILE)


def column_lane(r, t):
    return (t % PACK) * 32 + 2 * r


def pack_columns(packed, value, r, t):
    at = column_lane(r, t)
    lane = lanes_of(value.shape)
    here = (lane == at) | (lane == lax.rem(at + 127, 128))
    g = t // PACK
    packed[g] = jnp.where(here, pltpu.roll(value, at, 1), packed[g])


def join_columns(near, far, out):
    even = is_even("gy")
    for g in range(out.shape[0]):
        before = jnp.where(even, far[g], near[g])
        after = jnp.where(even, near[g], far[g])
        lane = lanes_of(before.shape)
        out[g] = jnp.where(lane % 2 == 0, pltpu.roll(before, 1, 1), pltpu.roll(after, 127, 1))


def along_lanes(value, columns, r, t):
    lane = lanes_of(value.shape)
    at = column_lane(r, t)
    edge = pltpu.roll(columns[t // PACK], lax.rem(128 - at, 128), 1)
    before = jnp.where(lane == 0, edge, pltpu.roll(value, 1, 1))
    after = jnp.where(lane == 127, edge, pltpu.roll(value, 127, 1))
    return before, after


def put_rows(near_rows, far_rows, t, value, first, last):
    even = is_even("gx")
    if first:
        far_rows[span(t), :] = jnp.where(even, value, far_rows[span(t), :])
        near_rows[span(t), :] = value
    if last:
        near_rows[span(t), :] = jnp.where(even, value, near_rows[span(t), :])
        far_rows[span(t), :] = jnp.where(even, far_rows[span(t), :], value)


def row_halo(near_rows, far_rows, t, upper):
    even = is_even("gx")
    near, far = near_rows[span(t), :], far_rows[span(t), :]
    return jnp.where(even, far, near) if upper else jnp.where(even, near, far)


def set_masks(sea, held, masks):
    sea, held = sea[...].astype(F32), held[...].astype(F32)
    masks[0] = sea * (1.0 - held)
    masks[1] = sea * held


def row_of(ref, r):
    return ref[pl.ds(r, 1), :]


def gathered(sums, q):
    rows = sums.shape[1] // TILE
    total = sums[q, pl.ds(0, rows, TILE), :]
    for k in range(1, TILE):
        total = total + sums[q, pl.ds(k, rows, TILE), :]
    return total


def block_of(lane):
    return lax.rem(lane + 1, 128) // 32


def edge_map(cell):
    lane = lanes_of((1, 128))
    packed = jnp.zeros((1, 128), F32)
    for r in range(cell.shape[0]):
        here = (lane == 2 * r) | (lane == (2 * r + 127) % 128)
        packed = jnp.where(here, pltpu.roll(cell[r : r + 1, :], 2 * r, 1), packed)
    out = packed
    for k in range(1, PACK):
        out = jnp.where(block_of(lane) == k, pltpu.roll(packed, 32 * k, 1), out)
    return out


def pick_group(values, g, tiles):
    block = block_of(lanes_of((TILE, 128)))
    out = jnp.broadcast_to(pick(values, g * PACK), block.shape)
    for k in range(1, min(PACK, tiles - g * PACK)):
        out = jnp.where(block == k, pick(values, g * PACK + k), out)
    return out


def edges_kernel(state, laid, near_rows, far_rows, cols, arrived):
    steps, rows, bins, lanes = laid.shape
    copies = [
        [pltpu.make_async_copy(state.at[s, :, r, :], laid.at[s, r], arrived.at[s, r]) for r in range(rows)]
        for s in range(steps)
    ]
    for r in range(rows):
        for s in range(steps):
            copies[s][r].start()
    packed = [[jnp.zeros((TILE, lanes), F32)] * cols.shape[1] for _ in range(steps)]
    for r in range(rows):
        if r % WAITS == 0:
            for s in range(steps):
                for copy in copies[s][r : r + WAITS]:
                    copy.wait()
        for s in range(steps):
            for t in range(bins // TILE):
                value = laid[s, r, span(t), :]
                pack_columns(packed[s], value, r, t)
                put_rows(near_rows.at[s], far_rows.at[s], t, value, r == 0, r == rows - 1)
    for s in range(steps):
        for g in range(cols.shape[1]):
            cols[s, g] = packed[s][g]


def prepare_kernel(local, growth, speed, code, seed, wind, coef, grown, edge_cols, laid, arrived):
    rows, bins, lanes = grown.shape
    copies = [pltpu.make_async_copy(seed.at[:, r, :], laid.at[r], arrived.at[r]) for r in range(rows)]
    for copy in copies:
        copy.start()

    def fill(d, carry):
        for f in range(local):
            x, y = speed[0, f, d], speed[1, f, d]
            next_x, next_y = lax.rem(code[f, d], 2) == 1, code[f, d] >= 2
            values = [
                1.0 - x - y,
                jnp.where(next_x, 0.0, x),
                jnp.where(next_x, x, 0.0),
                jnp.where(next_y, 0.0, y),
                jnp.where(next_y, y, 0.0),
                growth[f, d],
            ]
            for k, value in enumerate(values):
                coef[k, pl.ds(f * DIRS + d, 1), :] = jnp.full((1, lanes), value, F32)
        return carry

    lax.fori_loop(0, DIRS, fill, 0)
    packed = [jnp.zeros((TILE, lanes), F32)] * edge_cols.shape[0]
    for r in range(rows):
        if r % WAITS == 0:
            for copy in copies[r : r + WAITS]:
                copy.wait()
        half_wind = 0.5 * row_of(wind, r)
        for t in range(bins // TILE):
            value = laid[r, span(t), :] * jnp.exp(half_wind * coef[GROWTH, span(t), :])
            grown[r, span(t), :] = value
            pack_columns(packed, value, r, t)
    for g in range(edge_cols.shape[0]):
        edge_cols[g] = packed[g]


def moved_of(laid, near_rows, far_rows, columns, coef, s1, s2, r, t, first, last):
    value = laid[r, span(t), :]
    prev_x = row_halo(near_rows, far_rows, t, True) if first else laid[r - 1, span(t), :]
    next_x = row_halo(near_rows, far_rows, t, False) if last else laid[r + 1, span(t), :]
    prev_y, next_y = along_lanes(value, columns, r, t)
    flow = (
        coef[STAY, span(t), :] * value
        + coef[FROM_PREV_X, span(t), :] * prev_x
        + coef[FROM_NEXT_X, span(t), :] * next_x
        + coef[FROM_PREV_Y, span(t), :] * prev_y
        + coef[FROM_NEXT_Y, span(t), :] * next_y
    )
    return s1 * flow + s2 * value


def forward_row(local, coef, laid, grown, masks, halos, columns, sums, moved_0, r, first, last):
    bins = laid.shape[2]
    s1, s2 = row_of(masks.at[0], r), row_of(masks.at[1], r)
    parts = [[jnp.zeros((TILE, 128), F32)] * local for _ in range(4)]
    for t in range(bins // TILE):
        early, later = (
            moved_of(laid.at[s], *(h.at[s] for h in halos), columns.at[s], coef, s1, s2, r, t, first, last)
            for s in range(2)
        )
        moved_0[span(t), :] = early
        term = grown[r, span(t), :] * later
        values = later, early, term, coef[GROWTH, span(t), :] * term
        for part, value in zip(parts, values):
            accumulate(part, t, value)
    for i, part in enumerate(parts):
        for f in range(local):
            sums[i * local + f, tile_at(r), :] = part[f]


def forward_kernel(
    local, table, coef, laid, grown, sea, held, near_cols, far_cols, near_rows, far_rows,
    slots, wind_parts, moved_0, joined, masks, sums,
):
    _, rows, _, _ = laid.shape
    set_masks(sea, held, masks)
    for s in range(2):
        join_columns(near_cols.at[s], far_cols.at[s], joined.at[s])

    def body(r, first, last):
        halos = near_rows, far_rows
        forward_row(local, coef, laid, grown, masks, halos, joined, sums, moved_0.at[r], r, first, last)

    inner_rows(rows, body)
    outer_rows(rows, body)
    totals = [jnp.zeros((rows, 128), F32)] * 4
    for f in range(local):
        freq, weight = bin_constants(table, f, local)
        later, early = gathered(sums, f), gathered(sums, local + f)
        terms = weight * later, weight * freq * later, weight * early, weight * freq * early
        totals = [total + term for total, term in zip(totals, terms)]
        wind_parts[f] = gathered(sums, 3 * local + f)
    totals = totals + [gathered(sums, 2 * local + f) for f in range(local)]
    for i, value in enumerate(totals):
        for peer in range(slots.shape[0]):
            slots[peer, i] = value


def rates(energy, first):
    mean_freq = first / energy
    steep = steep_scale * energy * mean_freq**4
    inverse = 1.0 / (1.0 + steep)
    damping = (steep * inverse) ** 2
    q = damping / mean_freq
    return q, q / energy * (1.0 - 6.0 * inverse), q / first * (8.0 * inverse - 1.0)


def total_of(got, i):
    value = got[0, i]
    for peer in range(1, got.shape[0]):
        value = value + got[peer, i]
    return value


def lam_edges(local, table, grown, edge_cols, masks, q, by_energy, by_first, decays, rests, near_rows, far_rows, cols):
    rows, bins, _ = grown.shape
    packed_q, packed_energy, packed_first = edge_map(q), edge_map(by_energy), edge_map(by_first)
    packed_s1 = edge_map(masks[0])
    decay, rest = [], []
    for f in range(local):
        freq, weight = bin_constants(table, f, local)
        decays[f] = jnp.exp((-0.5 * freq) * q)
        rests[f] = weight * by_energy + (weight * freq) * by_first
        decay.append(jnp.exp((-0.5 * freq) * packed_q))
        rest.append(weight * packed_energy + (weight * freq) * packed_first)
    tiles = bins // TILE
    for g in range(cols.shape[0]):
        cols[g] = packed_s1 * (edge_cols[g] * pick_group(decay, g, tiles) + pick_group(rest, g, tiles))
    for r in (0, rows - 1):
        s1 = row_of(masks.at[0], r)
        decay = [row_of(decays.at[f], r) for f in range(local)]
        rest = [row_of(rests.at[f], r) for f in range(local)]
        for t in range(tiles):
            flow = s1 * (grown[r, span(t), :] * pick(decay, t) + pick(rest, t))
            put_rows(near_rows, far_rows, t, flow, r == 0, r > 0)


def lam_1_kernel(
    local, table, grown, edge_cols, sea, held, got, wind_parts,
    decays, rests, wind_1, cells, near_rows, far_rows, cols, masks,
):
    peers = got.shape[0]
    set_masks(sea, held, masks)
    q, by_energy, by_first = rates(1.0 + total_of(got, 0), 1.0 + total_of(got, 1))
    cells[0], cells[1], cells[2] = rates(1.0 + total_of(got, 2), 1.0 + total_of(got, 3))
    lam_q = jnp.zeros_like(q)
    for peer in range(peers):
        for f in range(local):
            freq = float(frequency_table[peer * local + f])
            lam_q = lam_q + (-0.5 * freq) * jnp.exp((-0.5 * freq) * q) * got[peer, 4 + f]
    by_energy, by_first = lam_q * by_energy, lam_q * by_first
    lam_edges(
        local, table, grown, edge_cols, masks, q, by_energy, by_first, decays, rests, near_rows, far_rows, cols
    )
    wind = jnp.zeros_like(q)
    for f in range(local):
        wind = wind + 0.5 * decays[f] * wind_parts[f]
    wind_1[...] = wind


def along_x_kernel(
    local, coef, grown, sea, held, decays, rests, near_rows, far_rows, flow, base, masks
):
    rows, bins, _ = grown.shape
    tiles = bins // TILE
    set_masks(sea, held, masks)

    def start(r):
        s1, s2 = row_of(masks.at[0], r), row_of(masks.at[1], r)
        decay = [row_of(decays.at[f], r) for f in range(local)]
        rest = [row_of(rests.at[f], r) for f in range(local)]
        for t in range(tiles):
            lam = grown[r, span(t), :] * pick(decay, t) + pick(rest, t)
            value = s1 * lam
            flow[r, span(t), :] = value
            base[r, span(t), :] = s2 * lam + coef[STAY, span(t), :] * value

    def start_pair(i, carry):
        start(2 * i)
        start(2 * i + 1)
        return carry

    lax.fori_loop(0, rows // 2, start_pair, 0)

    def body(r, first, last):
        for t in range(tiles):
            prev_x = row_halo(near_rows, far_rows, t, True) if first else flow[r - 1, span(t), :]
            next_x = row_halo(near_rows, far_rows, t, False) if last else flow[r + 1, span(t), :]
            base[r, span(t), :] = (
                base[r, span(t), :]
                + coef[FROM_NEXT_X, span(t), :] * prev_x
                + coef[FROM_PREV_X, span(t), :] * next_x
            )

    inner_rows(rows, body)
    outer_rows(rows, body)


def along_y(flow, base, columns, coef, r, t):
    prev_y, next_y = along_lanes(flow[r, span(t), :], columns, r, t)
    return (
        base[r, span(t), :]
        + coef[FROM_NEXT_Y, span(t), :] * prev_y
        + coef[FROM_PREV_Y, span(t), :] * next_y
    )


def set_decays(local, table, q, decays):
    for f in range(local):
        freq, _ = bin_constants(table, f, local)
        decay = jnp.exp((-0.5 * freq) * q)
        decays[f] = (-0.5 * freq) * decay
        decays[local + f] = 0.5 * decay


def back_1_kernel(
    local, table, coef, flow, base, moved_0, wind, cells, wind_1, near_cols, far_cols,
    grown, edge_cols, slots, joined, packed, decays, sums,
):
    rows, bins, _ = flow.shape
    join_columns(near_cols, far_cols, joined)
    set_decays(local, table, cells[0], decays)
    zero = jnp.zeros((TILE, 128), F32)
    groups = packed.shape[0]
    for g in range(groups):
        packed[g] = zero

    def row(r, columns):
        half_wind = 0.5 * row_of(wind, r)
        for_q = [row_of(decays.at[f], r) for f in range(local)]
        for_wind = [row_of(decays.at[local + f], r) for f in range(local)]
        lam_q = lam_wind = zero
        for t in range(bins // TILE):
            g = coef[GROWTH, span(t), :]
            density = along_y(flow, base, joined, coef, r, t) * jnp.exp(half_wind * g)
            grown[r, span(t), :] = density
            pack_columns(columns, density, r, t)
            term = density * moved_0[r, span(t), :]
            lam_q = lam_q + pick(for_q, t) * term
            lam_wind = lam_wind + pick(for_wind, t) * (g * term)
        sums[0, tile_at(r), :] = lam_q
        sums[1, tile_at(r), :] = lam_wind

    def pair(i, carry):
        columns = [packed[g] for g in range(groups)]
        row(2 * i, columns)
        row(2 * i + 1, columns)
        for g in range(groups):
            packed[g] = columns[g]
        return carry

    lax.fori_loop(0, rows // 2, pair, 0)
    for g in range(groups):
        edge_cols[g] = packed[g]
    lam_q, lam_wind = gathered(sums, 0), gathered(sums, 1) + wind_1[...]
    for peer in range(slots.shape[0]):
        slots[peer, 0] = lam_q
        slots[peer, 1] = lam_wind


def lam_0_kernel(
    local, table, grown, edge_cols, sea, held, cells, got, decays, rests, near_rows, far_rows, cols, masks
):
    set_masks(sea, held, masks)
    lam_q = total_of(got, 0)
    by_energy, by_first = lam_q * cells[1], lam_q * cells[2]
    lam_edges(
        local, table, grown, edge_cols, masks, cells[0], by_energy, by_first, decays, rests, near_rows, far_rows, cols
    )


def wind_kernel(got, wind_total):
    wind_total[...] = total_of(got, 1)


def back_0_kernel(coef, flow, base, near_cols, far_cols, out, joined, laid, sent):
    rows, bins, _ = flow.shape
    join_columns(near_cols, far_cols, joined)
    copies = [pltpu.make_async_copy(laid.at[r], out.at[:, r, :], sent.at[r]) for r in range(rows)]
    for r in range(rows):
        for t in range(bins // TILE):
            laid[r, span(t), :] = along_y(flow, base, joined, coef, r, t)
        copies[r].start()
    for copy in copies:
        copy.wait()


def swap(near, far, axis):
    count = lax.axis_size(axis)

    def pairs(first):
        return [(i + a, i + 1 - a) for i in range(first, count - 1, 2) for a in (0, 1)]

    return lax.ppermute(near, axis, pairs(0)), lax.ppermute(far, axis, pairs(1))


def exchange(near_rows, far_rows, cols):
    from_columns = swap(cols, cols, "gy")
    return from_columns, swap(near_rows, far_rows, "gx")


def call(body, outs, specs, *args, out_specs=None, scratch=(), us=2, mib=40):
    return pl.pallas_call(
        body,
        out_shape=[jax.ShapeDtypeStruct(shape, F32) for shape in outs],
        in_specs=specs,
        out_specs=out_specs or [VMEM] * len(outs),
        scratch_shapes=list(scratch),
        cost_estimate=pl.CostEstimate(flops=us * 1000000, bytes_accessed=us * 1000000, transcendentals=0),
        compiler_params=pltpu.CompilerParams(vmem_limit_bytes=mib * 1024 * 1024),
    )(*args)


def scratch(*shape):
    return pltpu.VMEM(shape, F32)


def shards(trajectory, adjoint_seed, wind, growth, speed, code, sea, held):
    steps, local, dirs, nx, ny = trajectory.shape
    bins = local * dirs
    peers = lax.axis_size("sa")
    groups = -(-bins // (TILE * PACK))
    table = jnp.asarray(np.stack([frequency_table, weight_table]))

    rows, cols, whole, cell = (bins, ny), (groups, TILE, ny), (nx, bins, ny), (nx, ny)
    edges = [rows, rows, cols]
    masks = scratch(2, *cell)

    sems, tiles = pltpu.SemaphoreType.DMA((nx,)), nx * TILE

    laid, *edge = call(
        edges_kernel,
        [(steps,) + shape for shape in [whole] + edges],
        [HBM],
        pltpu.with_memory_space_constraint(trajectory.reshape(steps, bins, nx, ny), pltpu.HBM),
        scratch=[pltpu.SemaphoreType.DMA((steps, nx))],
    )
    coef, grown, edge_cols = call(
        functools.partial(prepare_kernel, local),
        [(6,) + rows, whole, cols],
        [SMEM] * 3 + [HBM, VMEM],
        growth, speed, code, adjoint_seed.reshape(bins, nx, ny), wind,
        scratch=[scratch(*whole), sems],
    )
    from_columns, from_rows = exchange(*edge)
    slots, wind_parts, moved_0 = call(
        functools.partial(forward_kernel, local),
        [(peers, 4 + local) + cell, (local,) + cell, whole],
        [SMEM] + [VMEM] * 9,
        table, coef, laid, grown, sea, held, *from_columns, *from_rows,
        scratch=[scratch(steps, *cols), masks, scratch(4 * local, tiles, ny)],
        us=4,
    )
    got = lax.all_to_all(slots, "sa", 0, 0)
    by_freq = (local,) + cell
    decays, rests, wind_1, cells, *edge = call(
        functools.partial(lam_1_kernel, local),
        [by_freq, by_freq, cell, (3,) + cell] + edges,
        [SMEM] + [VMEM] * 6,
        table, grown, edge_cols, sea, held, got, wind_parts,
        scratch=[masks],
        us=1,
    )
    from_columns, from_rows = exchange(*edge)
    flow, base = call(
        functools.partial(along_x_kernel, local),
        [whole, whole],
        [VMEM] * 8,
        coef, grown, sea, held, decays, rests, *from_rows,
        scratch=[masks],
    )
    grown, edge_cols, slots = call(
        functools.partial(back_1_kernel, local),
        [whole, cols, (peers, 2) + cell],
        [SMEM] + [VMEM] * 9,
        table, coef, flow, base, moved_0, wind, cells, wind_1, *from_columns,
        scratch=[scratch(*cols), scratch(*cols), scratch(2 * local, *cell), scratch(2, tiles, ny)],
    )
    got = lax.all_to_all(slots, "sa", 0, 0)
    decays, rests, *edge = call(
        functools.partial(lam_0_kernel, local),
        [by_freq, by_freq] + edges,
        [SMEM] + [VMEM] * 6,
        table, grown, edge_cols, sea, held, cells, got,
        scratch=[masks],
        us=1,
    )
    from_columns, from_rows = exchange(*edge)
    flow, base = call(
        functools.partial(along_x_kernel, local),
        [whole, whole],
        [VMEM] * 8,
        coef, grown, sea, held, decays, rests, *from_rows,
        scratch=[masks],
    )
    (wind_total,) = call(wind_kernel, [cell], [VMEM], got, us=1)
    (out,) = call(
        back_0_kernel,
        [(bins, nx, ny)],
        [VMEM] * 5,
        coef, flow, base, *from_columns,
        out_specs=[HBM],
        scratch=[scratch(*cols), scratch(*whole), sems],
    )
    return out.reshape(local, dirs, nx, ny), wind_total


def solution(mesh):
    return jax.shard_map(
        shards,
        mesh=mesh,
        in_specs=(
            P(None, "sa", None, "gx", "gy"),
            P("sa", None, "gx", "gy"),
            P("gx", "gy"),
            P("sa", None),
            P(None, "sa", None),
            P("sa", None),
            P("gx", "gy"),
            P("gx", "gy"),
        ),
        out_specs=(P("sa", None, "gx", "gy"), P("gx", "gy")),
        check_vma=False,
    )
```

```python
import functools

import jax
import jax.numpy as jnp
import numpy as np
from jax import lax
from jax.experimental import pallas as pl
from jax.experimental.pallas import tpu as pltpu
from jax.sharding import PartitionSpec as P

FREQS = 32
DIRS = 36
TILE = 8
PACK = 4
WAITS = 4
F32 = jnp.float32

steep_scale = 0.05
freq_growth = 1.1

frequency_table = np.power(np.float32(freq_growth), np.arange(FREQS, dtype=np.float32) - FREQS // 2)
frequency_table = frequency_table.astype(np.float32)
weight_table = (frequency_table / np.sum(frequency_table) / np.float32(DIRS)).astype(np.float32)

VMEM = pl.BlockSpec(memory_space=pltpu.VMEM)
SMEM = pl.BlockSpec(memory_space=pltpu.SMEM)
HBM = pl.BlockSpec(memory_space=pltpu.HBM)

STAY, FROM_PREV_X, FROM_NEXT_X, FROM_PREV_Y, FROM_NEXT_Y, GROWTH, EDGE_Y, BACK_EDGE_Y = range(8)


def bin_constants(table, f, local):
    i = lax.axis_index("sa") * local + f
    return table[0, i], table[1, i]


def is_even(axis):
    return lax.rem(lax.axis_index(axis), 2) == 0


def span(t):
    return slice(t * TILE, (t + 1) * TILE)


def lanes_of(shape):
    return lax.broadcasted_iota(jnp.int32, shape, len(shape) - 1)


def tile_frequency(t):
    f = t * TILE // DIRS
    return f, (t * TILE + TILE - 1) // DIRS != f


def low_half():
    return lax.broadcasted_iota(jnp.int32, (TILE, 128), 0) < TILE // 2


def pick(values, t):
    f, mixed = tile_frequency(t)
    return jnp.where(low_half(), values[f], values[f + 1]) if mixed else values[f]


def accumulate(sums, t, value):
    f, mixed = tile_frequency(t)
    if mixed:
        low = low_half()
        sums[f] = sums[f] + jnp.where(low, value, 0.0)
        sums[f + 1] = sums[f + 1] + jnp.where(low, 0.0, value)
    else:
        sums[f] = sums[f] + value


def inner_rows(count, body):
    def pair(i, carry):
        body(2 * i + 1, False, False)
        body(2 * i + 2, False, False)
        return carry

    lax.fori_loop(0, (count - 2) // 2, pair, 0)


def outer_rows(count, body):
    body(0, True, False)
    body(count - 1, False, True)


def tile_at(r):
    at = r * TILE if isinstance(r, int) else pl.multiple_of(r * TILE, TILE)
    return pl.ds(at, TILE)


def column_lane(r, t):
    return (t % PACK) * 32 + 2 * r


def pack_columns(packed, value, r, t):
    at = column_lane(r, t)
    lane = lanes_of(value.shape)
    here = (lane == at) | (lane == lax.rem(at + 127, 128))
    g = t // PACK
    packed[g] = jnp.where(here, pltpu.roll(value, at, 1), packed[g])


def join_columns(near, far, out):
    even = is_even("gy")
    for g in range(out.shape[0]):
        before = jnp.where(even, far[g], near[g])
        after = jnp.where(even, near[g], far[g])
        lane = lanes_of(before.shape)
        out[g] = jnp.where(lane % 2 == 0, pltpu.roll(before, 1, 1), pltpu.roll(after, 127, 1))


def along_lanes(value):
    lane = lanes_of(value.shape)
    before = jnp.where(lane == 0, 0.0, pltpu.roll(value, 1, 1))
    after = jnp.where(lane == 127, 0.0, pltpu.roll(value, 127, 1))
    return before, after


def from_outside(columns, r, t):
    return pltpu.roll(columns[t // PACK], (128 - column_lane(r, t)) % 128, 1)


def put_rows(near_rows, far_rows, t, value, first, last):
    even = is_even("gx")
    if first:
        far_rows[span(t), :] = jnp.where(even, value, far_rows[span(t), :])
        near_rows[span(t), :] = value
    if last:
        near_rows[span(t), :] = jnp.where(even, value, near_rows[span(t), :])
        far_rows[span(t), :] = jnp.where(even, far_rows[span(t), :], value)


def row_halo(near_rows, far_rows, t, upper):
    even = is_even("gx")
    near, far = near_rows[span(t), :], far_rows[span(t), :]
    return jnp.where(even, far, near) if upper else jnp.where(even, near, far)


def set_masks(sea, held, masks):
    sea, held = sea[...].astype(F32), held[...].astype(F32)
    masks[0] = sea * (1.0 - held)
    masks[1] = sea * held


def row_of(ref, r):
    return ref[pl.ds(r, 1), :]


def gathered(sums, q):
    rows = sums.shape[1] // TILE
    total = sums[q, pl.ds(0, rows, TILE), :]
    for k in range(1, TILE):
        total = total + sums[q, pl.ds(k, rows, TILE), :]
    return total


def block_of(lane):
    return lax.rem(lane + 1, 128) // 32


def edge_map(cell):
    lane = lanes_of((1, 128))
    packed = jnp.zeros((1, 128), F32)
    for r in range(cell.shape[0]):
        here = (lane == 2 * r) | (lane == (2 * r + 127) % 128)
        packed = jnp.where(here, pltpu.roll(cell[r : r + 1, :], 2 * r, 1), packed)
    out = packed
    for k in range(1, PACK):
        out = jnp.where(block_of(lane) == k, pltpu.roll(packed, 32 * k, 1), out)
    return out


def pick_group(values, g, tiles):
    block = block_of(lanes_of((TILE, 128)))
    out = jnp.broadcast_to(pick(values, g * PACK), block.shape)
    for k in range(1, min(PACK, tiles - g * PACK)):
        out = jnp.where(block == k, pick(values, g * PACK + k), out)
    return out


def edges_kernel(state, laid, near_rows, far_rows, cols, arrived):
    steps, rows, bins, lanes = laid.shape
    copies = [
        [pltpu.make_async_copy(state.at[s, :, r, :], laid.at[s, r], arrived.at[s, r]) for r in range(rows)]
        for s in range(steps)
    ]
    for r in range(rows):
        for s in range(steps):
            copies[s][r].start()
    packed = [[jnp.zeros((TILE, lanes), F32)] * cols.shape[1] for _ in range(steps)]
    for r in range(rows):
        if r % WAITS == 0:
            for s in range(steps):
                for copy in copies[s][r : r + WAITS]:
                    copy.wait()
        for s in range(steps):
            for t in range(bins // TILE):
                value = laid[s, r, span(t), :]
                pack_columns(packed[s], value, r, t)
                put_rows(near_rows.at[s], far_rows.at[s], t, value, r == 0, r == rows - 1)
    for s in range(steps):
        for g in range(cols.shape[1]):
            cols[s, g] = packed[s][g]


def prepare_kernel(local, growth, speed, code, seed, wind, coef, grown, edge_cols, laid, arrived):
    rows, bins, lanes = grown.shape
    copies = [pltpu.make_async_copy(seed.at[:, r, :], laid.at[r], arrived.at[r]) for r in range(rows)]
    for copy in copies:
        copy.start()

    def fill(d, carry):
        for f in range(local):
            x, y = speed[0, f, d], speed[1, f, d]
            next_x, next_y = lax.rem(code[f, d], 2) == 1, code[f, d] >= 2
            values = [
                1.0 - x - y,
                jnp.where(next_x, 0.0, x),
                jnp.where(next_x, x, 0.0),
                jnp.where(next_y, 0.0, y),
                jnp.where(next_y, y, 0.0),
                growth[f, d],
            ]
            for k, value in enumerate(values):
                coef[k, pl.ds(f * DIRS + d, 1), :] = jnp.full((1, lanes), value, F32)
        return carry

    lax.fori_loop(0, DIRS, fill, 0)
    lane = lanes_of((TILE, lanes))
    for t in range(bins // TILE):
        before, after = coef[FROM_PREV_Y, span(t), :], coef[FROM_NEXT_Y, span(t), :]
        coef[EDGE_Y, span(t), :] = jnp.where(lane == 0, before, jnp.where(lane == 127, after, 0.0))
        coef[BACK_EDGE_Y, span(t), :] = jnp.where(lane == 0, after, jnp.where(lane == 127, before, 0.0))
    packed = [jnp.zeros((TILE, lanes), F32)] * edge_cols.shape[0]
    for r in range(rows):
        if r % WAITS == 0:
            for copy in copies[r : r + WAITS]:
                copy.wait()
        half_wind = 0.5 * row_of(wind, r)
        for t in range(bins // TILE):
            value = laid[r, span(t), :] * jnp.exp(half_wind * coef[GROWTH, span(t), :])
            grown[r, span(t), :] = value
            pack_columns(packed, value, r, t)
    for g in range(edge_cols.shape[0]):
        edge_cols[g] = packed[g]


def inner_forward_kernel(coef, laid, sea, held, near_rows, far_rows, base, masks):
    steps, rows, bins, _ = laid.shape
    set_masks(sea, held, masks)

    def body(r, first, last):
        s1, s2 = row_of(masks.at[0], r), row_of(masks.at[1], r)
        for s in range(steps):
            near, far = near_rows.at[s], far_rows.at[s]
            for t in range(bins // TILE):
                value = laid[s, r, span(t), :]
                prev_x = row_halo(near, far, t, True) if first else laid[s, r - 1, span(t), :]
                next_x = row_halo(near, far, t, False) if last else laid[s, r + 1, span(t), :]
                prev_y, next_y = along_lanes(value)
                flow = (
                    coef[STAY, span(t), :] * value
                    + coef[FROM_PREV_X, span(t), :] * prev_x
                    + coef[FROM_NEXT_X, span(t), :] * next_x
                    + coef[FROM_PREV_Y, span(t), :] * prev_y
                    + coef[FROM_NEXT_Y, span(t), :] * next_y
                )
                base[s, r, span(t), :] = s1 * flow + s2 * value

    inner_rows(rows, body)
    outer_rows(rows, body)


def forward_kernel(
    local, table, coef, base, grown, sea, held, far_cols, near_cols, slots, wind_parts, moved_0, joined, masks, sums
):
    steps, rows, bins, _ = base.shape
    set_masks(sea, held, masks)
    for s in range(steps):
        join_columns(near_cols.at[s], far_cols.at[s], joined.at[s])
    for r in range(rows):
        s1 = row_of(masks.at[0], r)
        parts = [[jnp.zeros((TILE, 128), F32)] * local for _ in range(4)]
        for t in range(bins // TILE):
            edge = s1 * coef[EDGE_Y, span(t), :]
            early, later = (
                base[s, r, span(t), :] + edge * from_outside(joined.at[s], r, t) for s in range(steps)
            )
            moved_0[r, span(t), :] = early
            term = grown[r, span(t), :] * later
            values = later, early, term, coef[GROWTH, span(t), :] * term
            for part, value in zip(parts, values):
                accumulate(part, t, value)
        for i, part in enumerate(parts):
            for f in range(local):
                sums[i * local + f, tile_at(r), :] = part[f]
    totals = [jnp.zeros((rows, 128), F32)] * 4
    for f in range(local):
        freq, weight = bin_constants(table, f, local)
        later, early = gathered(sums, f), gathered(sums, local + f)
        terms = weight * later, weight * freq * later, weight * early, weight * freq * early
        totals = [total + term for total, term in zip(totals, terms)]
        wind_parts[f] = gathered(sums, 3 * local + f)
    totals = totals + [gathered(sums, 2 * local + f) for f in range(local)]
    for i, value in enumerate(totals):
        for peer in range(slots.shape[0]):
            slots[peer, i] = value


def rates(energy, first):
    mean_freq = first / energy
    steep = steep_scale * energy * mean_freq**4
    inverse = 1.0 / (1.0 + steep)
    damping = (steep * inverse) ** 2
    q = damping / mean_freq
    return q, q / energy * (1.0 - 6.0 * inverse), q / first * (8.0 * inverse - 1.0)


def total_of(got, i):
    value = got[0, i]
    for peer in range(1, got.shape[0]):
        value = value + got[peer, i]
    return value


def lam_edges(local, table, grown, edge_cols, masks, q, by_energy, by_first, decays, rests, near_rows, far_rows, cols):
    rows, bins, _ = grown.shape
    packed_q, packed_energy, packed_first = edge_map(q), edge_map(by_energy), edge_map(by_first)
    packed_s1 = edge_map(masks[0])
    decay, rest = [], []
    for f in range(local):
        freq, weight = bin_constants(table, f, local)
        decays[f] = jnp.exp((-0.5 * freq) * q)
        rests[f] = weight * by_energy + (weight * freq) * by_first
        decay.append(jnp.exp((-0.5 * freq) * packed_q))
        rest.append(weight * packed_energy + (weight * freq) * packed_first)
    tiles = bins // TILE
    for g in range(cols.shape[0]):
        cols[g] = packed_s1 * (edge_cols[g] * pick_group(decay, g, tiles) + pick_group(rest, g, tiles))
    for r in (0, rows - 1):
        s1 = row_of(masks.at[0], r)
        decay = [row_of(decays.at[f], r) for f in range(local)]
        rest = [row_of(rests.at[f], r) for f in range(local)]
        for t in range(tiles):
            flow = s1 * (grown[r, span(t), :] * pick(decay, t) + pick(rest, t))
            put_rows(near_rows, far_rows, t, flow, r == 0, r > 0)


def lam_1_kernel(
    local, table, grown, edge_cols, sea, held, got, wind_parts,
    decays, rests, wind_1, cells, near_rows, far_rows, cols, masks,
):
    peers = got.shape[0]
    set_masks(sea, held, masks)
    q, by_energy, by_first = rates(1.0 + total_of(got, 0), 1.0 + total_of(got, 1))
    cells[0], cells[1], cells[2] = rates(1.0 + total_of(got, 2), 1.0 + total_of(got, 3))
    lam_q = jnp.zeros_like(q)
    for peer in range(peers):
        for f in range(local):
            freq = float(frequency_table[peer * local + f])
            lam_q = lam_q + (-0.5 * freq) * jnp.exp((-0.5 * freq) * q) * got[peer, 4 + f]
    by_energy, by_first = lam_q * by_energy, lam_q * by_first
    lam_edges(
        local, table, grown, edge_cols, masks, q, by_energy, by_first, decays, rests, near_rows, far_rows, cols
    )
    wind = jnp.zeros_like(q)
    for f in range(local):
        wind = wind + 0.5 * decays[f] * wind_parts[f]
    wind_1[...] = wind


def inner_back_kernel(
    local, coef, grown, sea, held, decays, rests, near_rows, far_rows, base, flow, masks
):
    rows, bins, _ = grown.shape
    tiles = bins // TILE
    set_masks(sea, held, masks)

    def start(r):
        s1, s2 = row_of(masks.at[0], r), row_of(masks.at[1], r)
        decay = [row_of(decays.at[f], r) for f in range(local)]
        rest = [row_of(rests.at[f], r) for f in range(local)]
        for t in range(tiles):
            lam = grown[r, span(t), :] * pick(decay, t) + pick(rest, t)
            value = s1 * lam
            flow[r, span(t), :] = value
            base[r, span(t), :] = s2 * lam + coef[STAY, span(t), :] * value

    def start_pair(i, carry):
        start(2 * i)
        start(2 * i + 1)
        return carry

    lax.fori_loop(0, rows // 2, start_pair, 0)

    def body(r, first, last):
        for t in range(tiles):
            prev_x = row_halo(near_rows, far_rows, t, True) if first else flow[r - 1, span(t), :]
            next_x = row_halo(near_rows, far_rows, t, False) if last else flow[r + 1, span(t), :]
            prev_y, next_y = along_lanes(flow[r, span(t), :])
            base[r, span(t), :] = (
                base[r, span(t), :]
                + coef[FROM_NEXT_X, span(t), :] * prev_x
                + coef[FROM_PREV_X, span(t), :] * next_x
                + coef[FROM_NEXT_Y, span(t), :] * prev_y
                + coef[FROM_PREV_Y, span(t), :] * next_y
            )

    inner_rows(rows, body)
    outer_rows(rows, body)


def complete(base, columns, coef, r, t):
    return base[r, span(t), :] + coef[BACK_EDGE_Y, span(t), :] * from_outside(columns, r, t)


def set_decays(local, table, q, decays):
    for f in range(local):
        freq, _ = bin_constants(table, f, local)
        decay = jnp.exp((-0.5 * freq) * q)
        decays[f] = (-0.5 * freq) * decay
        decays[local + f] = 0.5 * decay


def back_1_kernel(
    local, table, coef, base, moved_0, wind, cells, wind_1, far_cols, near_cols,
    grown, edge_cols, slots, joined, decays, sums,
):
    rows, bins, _ = base.shape
    join_columns(near_cols, far_cols, joined)
    set_decays(local, table, cells[0], decays)
    zero = jnp.zeros((TILE, 128), F32)
    packed = [zero] * edge_cols.shape[0]
    for r in range(rows):
        half_wind = 0.5 * row_of(wind, r)
        for_q = [row_of(decays.at[f], r) for f in range(local)]
        for_wind = [row_of(decays.at[local + f], r) for f in range(local)]
        lam_q = lam_wind = zero
        for t in range(bins // TILE):
            g = coef[GROWTH, span(t), :]
            density = complete(base, joined, coef, r, t) * jnp.exp(half_wind * g)
            grown[r, span(t), :] = density
            pack_columns(packed, density, r, t)
            term = density * moved_0[r, span(t), :]
            lam_q = lam_q + pick(for_q, t) * term
            lam_wind = lam_wind + pick(for_wind, t) * (g * term)
        sums[0, tile_at(r), :] = lam_q
        sums[1, tile_at(r), :] = lam_wind
    for g in range(edge_cols.shape[0]):
        edge_cols[g] = packed[g]
    lam_q, lam_wind = gathered(sums, 0), gathered(sums, 1) + wind_1[...]
    for peer in range(slots.shape[0]):
        slots[peer, 0] = lam_q
        slots[peer, 1] = lam_wind


def lam_0_kernel(
    local, table, grown, edge_cols, sea, held, cells, got, decays, rests, near_rows, far_rows, cols, masks
):
    set_masks(sea, held, masks)
    lam_q = total_of(got, 0)
    by_energy, by_first = lam_q * cells[1], lam_q * cells[2]
    lam_edges(
        local, table, grown, edge_cols, masks, cells[0], by_energy, by_first, decays, rests, near_rows, far_rows, cols
    )


def wind_kernel(got, wind_total):
    wind_total[...] = total_of(got, 1)


def back_0_kernel(coef, base, far_cols, near_cols, out, joined, laid, sent):
    rows, bins, _ = base.shape
    join_columns(near_cols, far_cols, joined)
    copies = [pltpu.make_async_copy(laid.at[r], out.at[:, r, :], sent.at[r]) for r in range(rows)]
    for r in range(rows):
        for t in range(bins // TILE):
            laid[r, span(t), :] = complete(base, joined, coef, r, t)
        copies[r].start()
    for copy in copies:
        copy.wait()


def swap(near, far, axis):
    count = lax.axis_size(axis)

    def pairs(first):
        return [(i + a, i + 1 - a) for i in range(first, count - 1, 2) for a in (0, 1)]

    if axis == "gy":
        far, near = lax.ppermute(far, axis, pairs(1)), lax.ppermute(near, axis, pairs(0))
    else:
        near, far = lax.ppermute(near, axis, pairs(0)), lax.ppermute(far, axis, pairs(1))
    return near, far


def exchange(near_rows, far_rows, cols):
    near_cols, far_cols = swap(cols, cols, "gy")
    return (far_cols, near_cols), swap(near_rows, far_rows, "gx")


def call(body, outs, specs, *args, out_specs=None, scratch=(), us=2, mib=40):
    return pl.pallas_call(
        body,
        out_shape=[jax.ShapeDtypeStruct(shape, F32) for shape in outs],
        in_specs=specs,
        out_specs=out_specs or [VMEM] * len(outs),
        scratch_shapes=list(scratch),
        cost_estimate=pl.CostEstimate(flops=us * 1000000, bytes_accessed=us * 1000000, transcendentals=0),
        compiler_params=pltpu.CompilerParams(vmem_limit_bytes=mib * 1024 * 1024),
    )(*args)


def scratch(*shape):
    return pltpu.VMEM(shape, F32)


def shards(trajectory, adjoint_seed, wind, growth, speed, code, sea, held):
    steps, local, dirs, nx, ny = trajectory.shape
    bins = local * dirs
    peers = lax.axis_size("sa")
    groups = -(-bins // (TILE * PACK))
    table = jnp.asarray(np.stack([frequency_table, weight_table]))

    rows, cols, whole, cell = (bins, ny), (groups, TILE, ny), (nx, bins, ny), (nx, ny)
    edges = [rows, rows, cols]
    masks = scratch(2, *cell)

    sems, tiles = pltpu.SemaphoreType.DMA((nx,)), nx * TILE

    laid, *edge = call(
        edges_kernel,
        [(steps,) + shape for shape in [whole] + edges],
        [HBM],
        pltpu.with_memory_space_constraint(trajectory.reshape(steps, bins, nx, ny), pltpu.HBM),
        scratch=[pltpu.SemaphoreType.DMA((steps, nx))],
    )
    coef, grown, edge_cols = call(
        functools.partial(prepare_kernel, local),
        [(8,) + rows, whole, cols],
        [SMEM] * 3 + [HBM, VMEM],
        growth, speed, code, adjoint_seed.reshape(bins, nx, ny), wind,
        scratch=[scratch(*whole), sems],
    )
    from_columns, from_rows = exchange(*edge)
    (base,) = call(
        inner_forward_kernel,
        [(steps,) + whole],
        [VMEM] * 6,
        coef, laid, sea, held, *from_rows,
        scratch=[masks],
    )
    slots, wind_parts, moved_0 = call(
        functools.partial(forward_kernel, local),
        [(peers, 4 + local) + cell, (local,) + cell, whole],
        [SMEM] + [VMEM] * 7,
        table, coef, base, grown, sea, held, *from_columns,
        scratch=[scratch(steps, *cols), masks, scratch(4 * local, tiles, ny)],
    )
    got = lax.all_to_all(slots, "sa", 0, 0)
    by_freq = (local,) + cell
    decays, rests, wind_1, cells, *edge = call(
        functools.partial(lam_1_kernel, local),
        [by_freq, by_freq, cell, (3,) + cell] + edges,
        [SMEM] + [VMEM] * 6,
        table, grown, edge_cols, sea, held, got, wind_parts,
        scratch=[masks],
        us=1,
    )
    from_columns, from_rows = exchange(*edge)
    (base,) = call(
        functools.partial(inner_back_kernel, local),
        [whole],
        [VMEM] * 8,
        coef, grown, sea, held, decays, rests, *from_rows,
        scratch=[scratch(*whole), masks],
    )
    grown, edge_cols, slots = call(
        functools.partial(back_1_kernel, local),
        [whole, cols, (peers, 2) + cell],
        [SMEM] + [VMEM] * 8,
        table, coef, base, moved_0, wind, cells, wind_1, *from_columns,
        scratch=[scratch(*cols), scratch(2 * local, *cell), scratch(2, tiles, ny)],
    )
    got = lax.all_to_all(slots, "sa", 0, 0)
    decays, rests, *edge = call(
        functools.partial(lam_0_kernel, local),
        [by_freq, by_freq] + edges,
        [SMEM] + [VMEM] * 6,
        table, grown, edge_cols, sea, held, cells, got,
        scratch=[masks],
        us=1,
    )
    from_columns, from_rows = exchange(*edge)
    (base,) = call(
        functools.partial(inner_back_kernel, local),
        [whole],
        [VMEM] * 8,
        coef, grown, sea, held, decays, rests, *from_rows,
        scratch=[scratch(*whole), masks],
    )
    (wind_total,) = call(wind_kernel, [cell], [VMEM], got, us=1)
    (out,) = call(
        back_0_kernel,
        [(bins, nx, ny)],
        [VMEM] * 4,
        coef, base, *from_columns,
        out_specs=[HBM],
        scratch=[scratch(*cols), scratch(*whole), sems],
    )
    return out.reshape(local, dirs, nx, ny), wind_total


def solution(mesh):
    return jax.shard_map(
        shards,
        mesh=mesh,
        in_specs=(
            P(None, "sa", None, "gx", "gy"),
            P("sa", None, "gx", "gy"),
            P("gx", "gy"),
            P("sa", None),
            P(None, "sa", None),
            P("sa", None),
            P("gx", "gy"),
            P("gx", "gy"),
        ),
        out_specs=(P("sa", None, "gx", "gy"), P("gx", "gy")),
        check_vma=False,
    )
```

```python
import functools

import jax
import jax.numpy as jnp
import numpy as np
from jax import lax
from jax.experimental import pallas as pl
from jax.experimental.pallas import tpu as pltpu
from jax.sharding import PartitionSpec as P

FREQS = 32
DIRS = 36
TILE = 8
PACK = 4
WAITS = 4
FILL = 4
F32 = jnp.float32

steep_scale = 0.05
freq_growth = 1.1

frequency_table = np.power(np.float32(freq_growth), np.arange(FREQS, dtype=np.float32) - FREQS // 2)
frequency_table = frequency_table.astype(np.float32)
weight_table = (frequency_table / np.sum(frequency_table) / np.float32(DIRS)).astype(np.float32)

VMEM = pl.BlockSpec(memory_space=pltpu.VMEM)
SMEM = pl.BlockSpec(memory_space=pltpu.SMEM)
HBM = pl.BlockSpec(memory_space=pltpu.HBM)

STAY, FROM_PREV_X, FROM_NEXT_X, FROM_PREV_Y, FROM_NEXT_Y, GROWTH, EDGE_Y, BACK_EDGE_Y = range(8)


def bin_constants(table, f, local):
    i = lax.axis_index("sa") * local + f
    return table[0, i], table[1, i]


def is_even(axis):
    return lax.rem(lax.axis_index(axis), 2) == 0


def span(t):
    return slice(t * TILE, (t + 1) * TILE)


def lanes_of(shape):
    return lax.broadcasted_iota(jnp.int32, shape, len(shape) - 1)


def tile_frequency(t):
    f = t * TILE // DIRS
    return f, (t * TILE + TILE - 1) // DIRS != f


def low_half():
    return lax.broadcasted_iota(jnp.int32, (TILE, 128), 0) < TILE // 2


def pick(values, t):
    f, mixed = tile_frequency(t)
    return jnp.where(low_half(), values[f], values[f + 1]) if mixed else values[f]


def accumulate(sums, t, value):
    f, mixed = tile_frequency(t)
    if mixed:
        low = low_half()
        sums[f] = sums[f] + jnp.where(low, value, 0.0)
        sums[f + 1] = sums[f + 1] + jnp.where(low, 0.0, value)
    else:
        sums[f] = sums[f] + value


def inner_rows(count, body):
    def pair(i, carry):
        body(2 * i + 1, False, False)
        body(2 * i + 2, False, False)
        return carry

    lax.fori_loop(0, (count - 2) // 2, pair, 0)


def outer_rows(count, body):
    body(0, True, False)
    body(count - 1, False, True)


def tile_at(r):
    at = r * TILE if isinstance(r, int) else pl.multiple_of(r * TILE, TILE)
    return pl.ds(at, TILE)


def column_lane(r, t):
    return (t % PACK) * 32 + 2 * r


def pack_columns(packed, value, r, t):
    at = column_lane(r, t)
    lane = lanes_of(value.shape)
    here = (lane == at) | (lane == lax.rem(at + 127, 128))
    g = t // PACK
    packed[g] = jnp.where(here, pltpu.roll(value, at, 1), packed[g])


def join_columns(near, far, out):
    even = is_even("gy")
    for g in range(out.shape[0]):
        before = jnp.where(even, far[g], near[g])
        after = jnp.where(even, near[g], far[g])
        lane = lanes_of(before.shape)
        out[g] = jnp.where(lane % 2 == 0, pltpu.roll(before, 1, 1), pltpu.roll(after, 127, 1))


def along_lanes(value):
    lane = lanes_of(value.shape)
    before = jnp.where(lane == 0, 0.0, pltpu.roll(value, 1, 1))
    after = jnp.where(lane == 127, 0.0, pltpu.roll(value, 127, 1))
    return before, after


def from_outside(columns, r, t):
    return pltpu.roll(columns[t // PACK], (128 - column_lane(r, t)) % 128, 1)


def put_rows(near_rows, far_rows, t, value, first, last):
    even = is_even("gx")
    if first:
        far_rows[span(t), :] = jnp.where(even, value, far_rows[span(t), :])
        near_rows[span(t), :] = value
    if last:
        near_rows[span(t), :] = jnp.where(even, value, near_rows[span(t), :])
        far_rows[span(t), :] = jnp.where(even, far_rows[span(t), :], value)


def row_halo(near_rows, far_rows, t, upper):
    even = is_even("gx")
    near, far = near_rows[span(t), :], far_rows[span(t), :]
    return jnp.where(even, far, near) if upper else jnp.where(even, near, far)


def set_masks(sea, held, masks):
    sea, held = sea[...].astype(F32), held[...].astype(F32)
    masks[0] = sea * (1.0 - held)
    masks[1] = sea * held


def row_of(ref, r):
    return ref[pl.ds(r, 1), :]


def gathered(sums, q):
    rows = sums.shape[1] // TILE
    total = sums[q, pl.ds(0, rows, TILE), :]
    for k in range(1, TILE):
        total = total + sums[q, pl.ds(k, rows, TILE), :]
    return total


def block_of(lane):
    return lax.rem(lane + 1, 128) // 32


def edge_map(cell):
    lane = lanes_of((1, 128))
    packed = jnp.zeros((1, 128), F32)
    for r in range(cell.shape[0]):
        here = (lane == 2 * r) | (lane == (2 * r + 127) % 128)
        packed = jnp.where(here, pltpu.roll(cell[r : r + 1, :], 2 * r, 1), packed)
    out = packed
    for k in range(1, PACK):
        out = jnp.where(block_of(lane) == k, pltpu.roll(packed, 32 * k, 1), out)
    return out


def pick_group(values, g, tiles):
    block = block_of(lanes_of((TILE, 128)))
    out = jnp.broadcast_to(pick(values, g * PACK), block.shape)
    for k in range(1, min(PACK, tiles - g * PACK)):
        out = jnp.where(block == k, pick(values, g * PACK + k), out)
    return out


def edges_kernel(state, laid, near_rows, far_rows, cols, arrived):
    steps, rows, bins, lanes = laid.shape
    copies = [
        [pltpu.make_async_copy(state.at[s, :, r, :], laid.at[s, r], arrived.at[s, r]) for r in range(rows)]
        for s in range(steps)
    ]
    for r in range(rows):
        for s in range(steps):
            copies[s][r].start()
    packed = [[jnp.zeros((TILE, lanes), F32)] * cols.shape[1] for _ in range(steps)]
    for r in range(rows):
        if r % WAITS == 0:
            for s in range(steps):
                for copy in copies[s][r : r + WAITS]:
                    copy.wait()
        for s in range(steps):
            for t in range(bins // TILE):
                value = laid[s, r, span(t), :]
                pack_columns(packed[s], value, r, t)
                put_rows(near_rows.at[s], far_rows.at[s], t, value, r == 0, r == rows - 1)
    for s in range(steps):
        for g in range(cols.shape[1]):
            cols[s, g] = packed[s][g]


def prepare_kernel(local, growth, speed, code, seed, wind, coef, grown, edge_cols, laid, arrived):
    rows, bins, lanes = grown.shape
    copies = [pltpu.make_async_copy(seed.at[:, r, :], laid.at[r], arrived.at[r]) for r in range(rows)]
    for copy in copies:
        copy.start()

    def fill(i, carry):
        for d, f in [(i * FILL + k, f) for k in range(FILL) for f in range(local)]:
            x, y = speed[0, f, d], speed[1, f, d]
            next_x, next_y = lax.rem(code[f, d], 2) == 1, code[f, d] >= 2
            values = [
                1.0 - x - y,
                jnp.where(next_x, 0.0, x),
                jnp.where(next_x, x, 0.0),
                jnp.where(next_y, 0.0, y),
                jnp.where(next_y, y, 0.0),
                growth[f, d],
            ]
            for k, value in enumerate(values):
                coef[k, pl.ds(f * DIRS + d, 1), :] = jnp.full((1, lanes), value, F32)
        return carry

    lax.fori_loop(0, DIRS // FILL, fill, 0)
    lane = lanes_of((TILE, lanes))
    for t in range(bins // TILE):
        before, after = coef[FROM_PREV_Y, span(t), :], coef[FROM_NEXT_Y, span(t), :]
        coef[EDGE_Y, span(t), :] = jnp.where(lane == 0, before, jnp.where(lane == 127, after, 0.0))
        coef[BACK_EDGE_Y, span(t), :] = jnp.where(lane == 0, after, jnp.where(lane == 127, before, 0.0))
    packed = [jnp.zeros((TILE, lanes), F32)] * edge_cols.shape[0]
    for r in range(rows):
        if r % WAITS == 0:
            for copy in copies[r : r + WAITS]:
                copy.wait()
        half_wind = 0.5 * row_of(wind, r)
        for t in range(bins // TILE):
            value = laid[r, span(t), :] * jnp.exp(half_wind * coef[GROWTH, span(t), :])
            grown[r, span(t), :] = value
            pack_columns(packed, value, r, t)
    for g in range(edge_cols.shape[0]):
        edge_cols[g] = packed[g]


def inner_forward_kernel(coef, laid, sea, held, near_rows, far_rows, base, masks):
    steps, rows, bins, _ = laid.shape
    set_masks(sea, held, masks)

    def body(r, first, last):
        s1, s2 = row_of(masks.at[0], r), row_of(masks.at[1], r)
        for s in range(steps):
            near, far = near_rows.at[s], far_rows.at[s]
            for t in range(bins // TILE):
                value = laid[s, r, span(t), :]
                prev_x = row_halo(near, far, t, True) if first else laid[s, r - 1, span(t), :]
                next_x = row_halo(near, far, t, False) if last else laid[s, r + 1, span(t), :]
                prev_y, next_y = along_lanes(value)
                flow = (
                    coef[STAY, span(t), :] * value
                    + coef[FROM_PREV_X, span(t), :] * prev_x
                    + coef[FROM_NEXT_X, span(t), :] * next_x
                    + coef[FROM_PREV_Y, span(t), :] * prev_y
                    + coef[FROM_NEXT_Y, span(t), :] * next_y
                )
                base[s, r, span(t), :] = s1 * flow + s2 * value

    inner_rows(rows, body)
    outer_rows(rows, body)


def forward_kernel(
    local, table, coef, base, grown, sea, held, far_cols, near_cols, slots, wind_parts, moved_0, joined, masks, sums
):
    steps, rows, bins, _ = base.shape
    set_masks(sea, held, masks)
    for s in range(steps):
        join_columns(near_cols.at[s], far_cols.at[s], joined.at[s])
    for r in range(rows):
        s1 = row_of(masks.at[0], r)
        parts = [[jnp.zeros((TILE, 128), F32)] * local for _ in range(4)]
        for t in range(bins // TILE):
            edge = s1 * coef[EDGE_Y, span(t), :]
            early, later = (
                base[s, r, span(t), :] + edge * from_outside(joined.at[s], r, t) for s in range(steps)
            )
            moved_0[r, span(t), :] = early
            term = grown[r, span(t), :] * later
            values = later, early, term, coef[GROWTH, span(t), :] * term
            for part, value in zip(parts, values):
                accumulate(part, t, value)
        for i, part in enumerate(parts):
            for f in range(local):
                sums[i * local + f, tile_at(r), :] = part[f]
    totals = [jnp.zeros((rows, 128), F32)] * 4
    for f in range(local):
        freq, weight = bin_constants(table, f, local)
        later, early = gathered(sums, f), gathered(sums, local + f)
        terms = weight * later, weight * freq * later, weight * early, weight * freq * early
        totals = [total + term for total, term in zip(totals, terms)]
        wind_parts[f] = gathered(sums, 3 * local + f)
    totals = totals + [gathered(sums, 2 * local + f) for f in range(local)]
    for i, value in enumerate(totals):
        for peer in range(slots.shape[0]):
            slots[peer, i] = value


def rates(energy, first):
    mean_freq = first / energy
    steep = steep_scale * energy * mean_freq**4
    inverse = 1.0 / (1.0 + steep)
    damping = (steep * inverse) ** 2
    q = damping / mean_freq
    return q, q / energy * (1.0 - 6.0 * inverse), q / first * (8.0 * inverse - 1.0)


def total_of(got, i):
    value = got[0, i]
    for peer in range(1, got.shape[0]):
        value = value + got[peer, i]
    return value


def lam_edges(local, table, grown, edge_cols, masks, q, by_energy, by_first, decays, rests, near_rows, far_rows, cols):
    rows, bins, _ = grown.shape
    packed_q, packed_energy, packed_first = edge_map(q), edge_map(by_energy), edge_map(by_first)
    packed_s1 = edge_map(masks[0])
    decay, rest = [], []
    for f in range(local):
        freq, weight = bin_constants(table, f, local)
        decays[f] = jnp.exp((-0.5 * freq) * q)
        rests[f] = weight * by_energy + (weight * freq) * by_first
        decay.append(jnp.exp((-0.5 * freq) * packed_q))
        rest.append(weight * packed_energy + (weight * freq) * packed_first)
    tiles = bins // TILE
    for g in range(cols.shape[0]):
        cols[g] = packed_s1 * (edge_cols[g] * pick_group(decay, g, tiles) + pick_group(rest, g, tiles))
    for r in (0, rows - 1):
        s1 = row_of(masks.at[0], r)
        decay = [row_of(decays.at[f], r) for f in range(local)]
        rest = [row_of(rests.at[f], r) for f in range(local)]
        for t in range(tiles):
            flow = s1 * (grown[r, span(t), :] * pick(decay, t) + pick(rest, t))
            put_rows(near_rows, far_rows, t, flow, r == 0, r > 0)


def lam_1_kernel(
    local, table, grown, edge_cols, sea, held, got, wind_parts,
    decays, rests, wind_1, cells, near_rows, far_rows, cols, masks,
):
    peers = got.shape[0]
    set_masks(sea, held, masks)
    q, by_energy, by_first = rates(1.0 + total_of(got, 0), 1.0 + total_of(got, 1))
    cells[0], cells[1], cells[2] = rates(1.0 + total_of(got, 2), 1.0 + total_of(got, 3))
    lam_q = jnp.zeros_like(q)
    for peer in range(peers):
        for f in range(local):
            freq = float(frequency_table[peer * local + f])
            lam_q = lam_q + (-0.5 * freq) * jnp.exp((-0.5 * freq) * q) * got[peer, 4 + f]
    by_energy, by_first = lam_q * by_energy, lam_q * by_first
    lam_edges(
        local, table, grown, edge_cols, masks, q, by_energy, by_first, decays, rests, near_rows, far_rows, cols
    )
    wind = jnp.zeros_like(q)
    for f in range(local):
        wind = wind + 0.5 * decays[f] * wind_parts[f]
    wind_1[...] = wind


def inner_back_kernel(
    local, coef, grown, sea, held, decays, rests, near_rows, far_rows, base, flow, masks
):
    rows, bins, _ = grown.shape
    tiles = bins // TILE
    set_masks(sea, held, masks)

    def start(r):
        s1, s2 = row_of(masks.at[0], r), row_of(masks.at[1], r)
        decay = [row_of(decays.at[f], r) for f in range(local)]
        rest = [row_of(rests.at[f], r) for f in range(local)]
        for t in range(tiles):
            lam = grown[r, span(t), :] * pick(decay, t) + pick(rest, t)
            value = s1 * lam
            flow[r, span(t), :] = value
            base[r, span(t), :] = s2 * lam + coef[STAY, span(t), :] * value

    def start_pair(i, carry):
        start(2 * i)
        start(2 * i + 1)
        return carry

    lax.fori_loop(0, rows // 2, start_pair, 0)

    def body(r, first, last):
        for t in range(tiles):
            prev_x = row_halo(near_rows, far_rows, t, True) if first else flow[r - 1, span(t), :]
            next_x = row_halo(near_rows, far_rows, t, False) if last else flow[r + 1, span(t), :]
            prev_y, next_y = along_lanes(flow[r, span(t), :])
            base[r, span(t), :] = (
                base[r, span(t), :]
                + coef[FROM_NEXT_X, span(t), :] * prev_x
                + coef[FROM_PREV_X, span(t), :] * next_x
                + coef[FROM_NEXT_Y, span(t), :] * prev_y
                + coef[FROM_PREV_Y, span(t), :] * next_y
            )

    inner_rows(rows, body)
    outer_rows(rows, body)


def complete(base, columns, coef, r, t):
    return base[r, span(t), :] + coef[BACK_EDGE_Y, span(t), :] * from_outside(columns, r, t)


def set_decays(local, table, q, decays):
    for f in range(local):
        freq, _ = bin_constants(table, f, local)
        decay = jnp.exp((-0.5 * freq) * q)
        decays[f] = (-0.5 * freq) * decay
        decays[local + f] = 0.5 * decay


def back_1_kernel(
    local, table, coef, base, moved_0, wind, cells, wind_1, far_cols, near_cols,
    grown, edge_cols, slots, joined, decays, sums,
):
    rows, bins, _ = base.shape
    join_columns(near_cols, far_cols, joined)
    set_decays(local, table, cells[0], decays)
    zero = jnp.zeros((TILE, 128), F32)
    packed = [zero] * edge_cols.shape[0]
    for r in range(rows):
        half_wind = 0.5 * row_of(wind, r)
        for_q = [row_of(decays.at[f], r) for f in range(local)]
        for_wind = [row_of(decays.at[local + f], r) for f in range(local)]
        lam_q = lam_wind = zero
        for t in range(bins // TILE):
            g = coef[GROWTH, span(t), :]
            density = complete(base, joined, coef, r, t) * jnp.exp(half_wind * g)
            grown[r, span(t), :] = density
            pack_columns(packed, density, r, t)
            term = density * moved_0[r, span(t), :]
            lam_q = lam_q + pick(for_q, t) * term
            lam_wind = lam_wind + pick(for_wind, t) * (g * term)
        sums[0, tile_at(r), :] = lam_q
        sums[1, tile_at(r), :] = lam_wind
    for g in range(edge_cols.shape[0]):
        edge_cols[g] = packed[g]
    lam_q, lam_wind = gathered(sums, 0), gathered(sums, 1) + wind_1[...]
    for peer in range(slots.shape[0]):
        slots[peer, 0] = lam_q
        slots[peer, 1] = lam_wind


def lam_0_kernel(
    local, table, grown, edge_cols, sea, held, cells, got, decays, rests, near_rows, far_rows, cols, masks
):
    set_masks(sea, held, masks)
    lam_q = total_of(got, 0)
    by_energy, by_first = lam_q * cells[1], lam_q * cells[2]
    lam_edges(
        local, table, grown, edge_cols, masks, cells[0], by_energy, by_first, decays, rests, near_rows, far_rows, cols
    )


def back_0_kernel(coef, base, far_cols, near_cols, out, joined, laid, sent):
    rows, bins, _ = base.shape
    join_columns(near_cols, far_cols, joined)
    copies = [pltpu.make_async_copy(laid.at[r], out.at[:, r, :], sent.at[r]) for r in range(rows)]
    for r in range(rows):
        for t in range(bins // TILE):
            laid[r, span(t), :] = complete(base, joined, coef, r, t)
        copies[r].start()
    for copy in copies:
        copy.wait()


def swap(near, far, axis):
    count = lax.axis_size(axis)

    def pairs(first):
        return [(i + a, i + 1 - a) for i in range(first, count - 1, 2) for a in (0, 1)]

    if axis == "gy":
        far, near = lax.ppermute(far, axis, pairs(1)), lax.ppermute(near, axis, pairs(0))
    else:
        near, far = lax.ppermute(near, axis, pairs(0)), lax.ppermute(far, axis, pairs(1))
    return near, far


def exchange(near_rows, far_rows, cols):
    near_cols, far_cols = swap(cols, cols, "gy")
    return (far_cols, near_cols), swap(near_rows, far_rows, "gx")


def call(body, outs, specs, *args, out_specs=None, scratch=(), us=2, mib=40):
    return pl.pallas_call(
        body,
        out_shape=[jax.ShapeDtypeStruct(shape, F32) for shape in outs],
        in_specs=specs,
        out_specs=out_specs or [VMEM] * len(outs),
        scratch_shapes=list(scratch),
        cost_estimate=pl.CostEstimate(flops=us * 1000000, bytes_accessed=us * 1000000, transcendentals=0),
        compiler_params=pltpu.CompilerParams(vmem_limit_bytes=mib * 1024 * 1024),
    )(*args)


def scratch(*shape):
    return pltpu.VMEM(shape, F32)


def shards(trajectory, adjoint_seed, wind, growth, speed, code, sea, held):
    steps, local, dirs, nx, ny = trajectory.shape
    bins = local * dirs
    peers = lax.axis_size("sa")
    groups = -(-bins // (TILE * PACK))
    table = jnp.asarray(np.stack([frequency_table, weight_table]))

    rows, cols, whole, cell = (bins, ny), (groups, TILE, ny), (nx, bins, ny), (nx, ny)
    edges = [rows, rows, cols]
    masks = scratch(2, *cell)

    sems, tiles = pltpu.SemaphoreType.DMA((nx,)), nx * TILE

    laid, *edge = call(
        edges_kernel,
        [(steps,) + shape for shape in [whole] + edges],
        [HBM],
        pltpu.with_memory_space_constraint(trajectory.reshape(steps, bins, nx, ny), pltpu.HBM),
        scratch=[pltpu.SemaphoreType.DMA((steps, nx))],
    )
    coef, grown, edge_cols = call(
        functools.partial(prepare_kernel, local),
        [(8,) + rows, whole, cols],
        [SMEM] * 3 + [HBM, VMEM],
        growth, speed, code, adjoint_seed.reshape(bins, nx, ny), wind,
        scratch=[scratch(*whole), sems],
    )
    from_columns, from_rows = exchange(*edge)
    (base,) = call(
        inner_forward_kernel,
        [(steps,) + whole],
        [VMEM] * 6,
        coef, laid, sea, held, *from_rows,
        scratch=[masks],
    )
    slots, wind_parts, moved_0 = call(
        functools.partial(forward_kernel, local),
        [(peers, 4 + local) + cell, (local,) + cell, whole],
        [SMEM] + [VMEM] * 7,
        table, coef, base, grown, sea, held, *from_columns,
        scratch=[scratch(steps, *cols), masks, scratch(4 * local, tiles, ny)],
    )
    got = lax.all_to_all(slots, "sa", 0, 0)
    by_freq = (local,) + cell
    decays, rests, wind_1, cells, *edge = call(
        functools.partial(lam_1_kernel, local),
        [by_freq, by_freq, cell, (3,) + cell] + edges,
        [SMEM] + [VMEM] * 6,
        table, grown, edge_cols, sea, held, got, wind_parts,
        scratch=[masks],
        us=1,
    )
    from_columns, from_rows = exchange(*edge)
    (base,) = call(
        functools.partial(inner_back_kernel, local),
        [whole],
        [VMEM] * 8,
        coef, grown, sea, held, decays, rests, *from_rows,
        scratch=[scratch(*whole), masks],
    )
    grown, edge_cols, slots = call(
        functools.partial(back_1_kernel, local),
        [whole, cols, (peers, 2) + cell],
        [SMEM] + [VMEM] * 8,
        table, coef, base, moved_0, wind, cells, wind_1, *from_columns,
        scratch=[scratch(*cols), scratch(2 * local, *cell), scratch(2, tiles, ny)],
    )
    got = lax.all_to_all(slots, "sa", 0, 0)
    decays, rests, *edge = call(
        functools.partial(lam_0_kernel, local),
        [by_freq, by_freq] + edges,
        [SMEM] + [VMEM] * 6,
        table, grown, edge_cols, sea, held, cells, got,
        scratch=[masks],
        us=1,
    )
    from_columns, from_rows = exchange(*edge)
    (base,) = call(
        functools.partial(inner_back_kernel, local),
        [whole],
        [VMEM] * 8,
        coef, grown, sea, held, decays, rests, *from_rows,
        scratch=[scratch(*whole), masks],
    )
    got, base = lax.optimization_barrier((got, base))
    wind_total = jnp.sum(got[:, 1], axis=0)
    (out,) = call(
        back_0_kernel,
        [(bins, nx, ny)],
        [VMEM] * 4,
        coef, base, *from_columns,
        out_specs=[HBM],
        scratch=[scratch(*cols), scratch(*whole), sems],
    )
    return out.reshape(local, dirs, nx, ny), wind_total


def solution(mesh):
    return jax.shard_map(
        shards,
        mesh=mesh,
        in_specs=(
            P(None, "sa", None, "gx", "gy"),
            P("sa", None, "gx", "gy"),
            P("gx", "gy"),
            P("sa", None),
            P(None, "sa", None),
            P("sa", None),
            P("gx", "gy"),
            P("gx", "gy"),
        ),
        out_specs=(P("sa", None, "gx", "gy"), P("gx", "gy")),
        check_vma=False,
    )
```
